32 devices in a mesh: win: 8 (over z, x), frm: 4 (over y, core).
Axes of the slice: x: 2, y: 2, z: 4, core: 2. Of those that a mesh axis runs over, the one named last changes fastest.
Arguments:
- hidden_state: bfloat16 [8192, 1536], P(('win', 'frm')), may hold values from -600 to 600
- latent: float32 [8192, 64], P(('win', 'frm')), may hold values from -6 to 6
- stale_kv: bfloat16 [8192, 1536], P(('win', 'frm')), may hold values from -100 to 100
- mod_shift: float32 [8, 1536], P('win'), may hold values from -3 to 3
- mod_scale: float32 [8, 1536], P('win'), may hold values from -3 to 3
- mod_gate: float32 [8, 1536], P('win'), may hold values from 0.5 to 4
- w_query: bfloat16 [1536, 768], replicated, may hold values from -0.29882812 to 0.29882812
- w_keyval: bfloat16 [1536, 1536], replicated, may hold values from -0.15625 to 0.15625
- w_out: bfloat16 [768, 1536], replicated, may hold values from -0.21875 to 0.21875
- w_final: bfloat16 [1536, 64], replicated, may hold values from -0.15625 to 0.15625
- step_size: float32 [8], P('win'), may hold values from 0.5 to 1.5
Outputs:
- next_latent: float32 [8192, 64], P(('win', 'frm'))
The draws below stay inside these ranges and needn't reach their ends.
All inputs are finite; a program needn't handle non-finite values.
Results may differ from the reference program's by a relative error of at most 0.0024.
Values may be sent and summed in bfloat16 or wider, within the bound.
A program may use at most 192 MiB of HBM per device.

```python
import math
import jax
import jax.numpy as jnp
from jax import lax

D = 1536
HEADS = 12
HEAD_DIM = 64
CH = 64
F_DEV = 256
QW = 768
FRAMES = 1024
SEAM = 512
WINS = 8
N_FRM = 4


def draw_hidden_state(key, part):
    noise_key, column_key = jax.random.split(key, 2)
    total_rows = WINS * FRAMES
    values = jnp.clip(jax.random.normal(noise_key, (total_rows, D), jnp.float32), -6.0, 6.0)
    column_scale = jnp.exp(jax.random.uniform(column_key, (1, D), jnp.float32, 0.0, math.log(10.0)))
    values = values * column_scale
    return values.astype(jnp.bfloat16)


def draw_stale_kv(key, part):
    noise_key = jax.random.fold_in(key, 0)
    total_rows = WINS * FRAMES
    query_width = HEADS * HEAD_DIM
    values = jnp.clip(jax.random.normal(noise_key, (total_rows, 2 * query_width), jnp.float32), -6.0, 6.0)
    return values.astype(jnp.bfloat16)


def shard_levels(rng, dims, cuts, least, top_value):
    gain = 1.0
    for position, blocks in cuts:
        draws = jax.random.uniform(jax.random.fold_in(jax.random.fold_in(rng, 6), position), (blocks,), jnp.float32, least / len(cuts), top_value / len(cuts))
        gain = gain * jnp.repeat(jnp.exp(draws), dims[position] // blocks).reshape((-1,) + (1,) * (len(dims) - 1 - position))
    return gain


def normal_values(stream_key, dims, spread, limit, shards=(), kind=jnp.bfloat16):
    drawn = spread * jax.random.normal(stream_key, dims, jnp.float32)
    if shards:
        drawn = drawn * shard_levels(stream_key, dims, shards, -0.22, 0.18)
    return jnp.clip(drawn, -limit, limit).astype(kind)


def setup_inputs(seed: int = 0) -> dict:
    keys = jax.random.split(jax.random.key(seed), 12)
    return {
        "hidden_state": draw_hidden_state(jax.random.fold_in(keys[11], 71), 0),
        "latent": normal_values(keys[1], (WINS * FRAMES, CH), 1.0, 6.0, ((0, 32),), jnp.float32),
        "stale_kv": draw_stale_kv(jax.random.fold_in(keys[11], 71), 0),
        "mod_shift": normal_values(keys[3], (WINS, D), 0.5, 3.0, ((0, 8),), jnp.float32),
        "mod_scale": normal_values(keys[4], (WINS, D), 0.5, 3.0, ((0, 8),), jnp.float32),
        "mod_gate": jnp.clip(jnp.exp(math.log(4.0) - 2.0794415 * jax.random.uniform(keys[5], (WINS, D), jnp.float32) ** shard_levels(keys[5], (WINS, D), ((0, 8),), -0.2, 0.2)), 0.5, 4.0),
        "w_query": normal_values(keys[6], (D, QW), 0.05, 0.29882812),
        "w_keyval": normal_values(keys[7], (D, 2 * QW), D ** -0.5, 0.15625),
        "w_out": normal_values(keys[8], (QW, D), QW ** -0.5, 0.21875),
        "w_final": normal_values(keys[9], (D, CH), D ** -0.5, 0.15625),
        "step_size": jnp.clip(0.5 + 1.0 * jax.random.uniform(keys[10], (WINS,), jnp.float32) ** shard_levels(keys[10], (WINS,), ((0, 8),), -0.2, 0.2), 0.5, 1.5),
    }


def layer_norm(values):
    average = lax.optimization_barrier(jnp.mean(values, axis=-1, keepdims=True))
    centred = values - average
    variance = lax.optimization_barrier(jnp.mean(centred * centred, axis=-1, keepdims=True))
    return centred * lax.rsqrt(variance + 1e-06)

def reference(hidden_state, latent, stale_kv, mod_shift, mod_scale, mod_gate, w_query, w_keyval, w_out, w_final, step_size):
    query_width = HEADS * HEAD_DIM
    scale_factor = HEAD_DIM ** (-0.5)

    def window_update(inputs):
        window_hidden, window_latent, window_kv, shift_row, scale_row, gate_row, window_step = inputs
        stream = window_hidden.astype(jnp.float32)
        modulated = (layer_norm(stream) * (1.0 + scale_row) + shift_row).astype(jnp.bfloat16)
        queries = jnp.dot(modulated, w_query, preferred_element_type=jnp.float32).astype(jnp.bfloat16)
        fresh_kv = jnp.dot(modulated, w_keyval, preferred_element_type=jnp.float32).astype(jnp.bfloat16)

        def frame_block(block_id):
            block_start = (block_id * F_DEV).astype(jnp.int32)
            fresh_rows = lax.dynamic_slice_in_dim(fresh_kv, block_start, F_DEV, 0)
            key_value = lax.dynamic_update_slice_in_dim(window_kv, fresh_rows, block_start, 0)
            query_heads = lax.dynamic_slice_in_dim(queries, block_start, F_DEV, 0)
            query_heads = query_heads.reshape(F_DEV, HEADS, HEAD_DIM).astype(jnp.float32)
            key_rows = key_value[:, :query_width].reshape(FRAMES, HEADS, HEAD_DIM).astype(jnp.float32)
            value_rows = key_value[:, query_width:].reshape(FRAMES, HEADS, HEAD_DIM).astype(jnp.float32)
            scores = jnp.einsum('qhd,khd->hqk', query_heads, key_rows) * scale_factor
            row_max = lax.optimization_barrier(jnp.max(scores, axis=-1, keepdims=True))
            probs = jnp.exp(scores - row_max)
            totals = lax.optimization_barrier(jnp.sum(probs, axis=-1))
            weights = lax.optimization_barrier(probs.astype(jnp.bfloat16)).astype(jnp.float32)
            summed = jnp.einsum('hqk,khd->qhd', weights, value_rows)
            attended = summed / jnp.transpose(totals)[:, :, None]
            return attended.reshape(F_DEV, query_width).astype(jnp.bfloat16)
        attention = lax.map(frame_block, jnp.arange(N_FRM, dtype=jnp.int32)).reshape(FRAMES, query_width)
        combined = stream + gate_row * jnp.dot(attention, w_out, preferred_element_type=jnp.float32)
        normed = layer_norm(combined).astype(jnp.bfloat16)
        velocity = jnp.dot(normed, w_final, preferred_element_type=jnp.float32)
        return window_latent + window_step * velocity
    advanced = lax.map(window_update, (hidden_state.reshape(WINS, FRAMES, D), latent.reshape(WINS, FRAMES, CH), stale_kv.reshape(WINS, FRAMES, 2 * query_width), mod_shift, mod_scale, mod_gate, step_size))
    ramp_up = ((jnp.arange(SEAM, dtype=jnp.float32) + 0.5) / SEAM)[:, None]
    tail_rows = advanced[:-1, FRAMES - SEAM:]
    head_rows = advanced[1:, :SEAM]
    blended = (1.0 - ramp_up) * tail_rows + ramp_up * head_rows
    advanced = advanced.at[:-1, FRAMES - SEAM:].set(blended)
    advanced = advanced.at[1:, :SEAM].set(blended)
    return advanced.reshape(WINS * FRAMES, CH)
```

```python
import functools

import jax
import jax.numpy as jnp
from jax import lax
from jax.experimental import pallas as pl
from jax.experimental.pallas import tpu as pltpu
from jax.sharding import PartitionSpec as P

HEAD_DIM = 64
PAIR = 2 * HEAD_DIM
TILE = 256
LN_ROWS = 32
MESH = pl.DeviceIdType.MESH
NT = (((1,), (1,)), ((), ()))


def layer_norm(values):
    average = jnp.mean(values, axis=-1, keepdims=True)
    centred = values - average
    variance = jnp.mean(centred * centred, axis=-1, keepdims=True)
    return centred * lax.rsqrt(variance + 1e-06)


def kernel(
    windows,
    frame_devs,
    step_ref,
    hidden_hbm,
    latent_hbm,
    stale_hbm,
    shift_hbm,
    scale_hbm,
    gate_hbm,
    wq_hbm,
    wkv_hbm,
    wo_hbm,
    wf_hbm,
    out_ref,
    hidden,
    latent,
    shift,
    scale,
    gate,
    wq,
    wkv,
    wo,
    wf,
    modulated,
    queries,
    kv,
    attention,
    combined,
    normed,
    advanced,
    other,
    load_sem,
    send_sem,
    recv_sem,
    seam_send,
    seam_recv,
):
    rows, width = hidden.shape
    qw = queries.shape[1]
    pairs = qw // PAIR
    chips = frame_devs // 2
    half_devs = frame_devs // 2
    w = lax.axis_index("win")
    f = lax.axis_index("frm")
    chip, core = f // 2, f % 2
    sibling = (w, chip * 2 + (1 - core))
    peers = [(w, ((chip + j) % chips) * 2 + core) for j in range(1, chips)]
    in_tail = f >= half_devs
    has_partner = jnp.where(in_tail, w < windows - 1, w > 0)
    partner = (
        jnp.where(in_tail, w + 1, w - 1),
        jnp.where(in_tail, f - half_devs, f + half_devs),
    )

    loads = [
        pltpu.make_async_copy(src, dst, load_sem.at[i])
        for i, (src, dst) in enumerate(
            [
                (hidden_hbm, hidden),
                (scale_hbm, scale),
                (shift_hbm, shift),
                (wq_hbm, wq),
                (wkv_hbm.at[:, pl.ds(0, qw)], wkv.at[:, pl.ds(0, qw)]),
                (wkv_hbm.at[:, pl.ds(qw, qw)], wkv.at[:, pl.ds(qw, qw)]),
                (gate_hbm, gate),
                (wo_hbm, wo),
                (wf_hbm, wf),
                (latent_hbm, latent),
            ]
        )
    ]
    for load in loads:
        load.start()

    barrier = pltpu.get_barrier_semaphore()
    for device in [sibling] + peers:
        pl.semaphore_signal(barrier, inc=1, device_id=device, device_id_type=MESH)

    @pl.when(has_partner)
    def _():
        pl.semaphore_signal(barrier, inc=1, device_id=partner, device_id_type=MESH)

    pl.semaphore_wait(barrier, jnp.where(has_partner, chips + 1, chips))

    def columns(g, part):
        return pl.ds(pl.multiple_of(part * qw + g * PAIR, PAIR), PAIR)

    def send(source, slot, device, g, part):
        return pltpu.make_async_remote_copy(
            src_ref=source.at[:, columns(g, part)],
            dst_ref=kv.at[pl.ds(slot * rows, rows), columns(g, part)],
            send_sem=send_sem.at[slot, g, part],
            recv_sem=recv_sem.at[slot, g, part],
            device_id=device,
            device_id_type=MESH,
        )

    def to_sibling(g, part):
        return send(stale_hbm, 1, sibling, g, part)

    def to_peer(j, g, part):
        return send(stale_hbm, 2 * j, peers[j - 1], g, part)

    def forward(j, g, part):
        return send(kv.at[pl.ds(2 * j * rows, rows)], 2 * j + 1, sibling, g, part)

    @pl.loop(0, pairs)
    def _(g):
        for part in range(2):
            for j in range(1, chips):
                to_peer(j, g, part).start()
            to_sibling(g, part).start()

    def arrive(g):
        for j in range(1, chips):
            for part in range(2):
                to_peer(j, g, part).wait_recv()
                forward(j, g, part).start()

    def ready(g):
        for part in range(2):
            to_sibling(g, part).wait_recv()
            for j in range(1, chips):
                forward(j, g, part).wait_recv()

    for load in loads[:3]:
        load.wait()

    @pl.loop(0, rows // LN_ROWS)
    def _(i):
        at = pl.ds(pl.multiple_of(i * LN_ROWS, LN_ROWS), LN_ROWS)
        line = layer_norm(hidden[at, :].astype(jnp.float32))
        modulated[at, :] = (line * (1.0 + scale[...]) + shift[...]).astype(jnp.bfloat16)

    loads[3].wait()

    @pl.loop(0, qw // TILE)
    def _(i):
        at = pl.ds(pl.multiple_of(i * TILE, TILE), TILE)
        tile = jnp.dot(modulated[...], wq[:, at], preferred_element_type=jnp.float32)
        queries[:, at] = (tile * HEAD_DIM ** (-0.5)).astype(jnp.bfloat16)

    loads[4].wait()
    loads[5].wait()

    @pl.loop(0, 2 * qw // TILE)
    def _(i):
        at = pl.ds(pl.multiple_of(i * TILE, TILE), TILE)
        tile = jnp.dot(modulated[...], wkv[:, at], preferred_element_type=jnp.float32)
        kv[pl.ds(0, rows), at] = tile.astype(jnp.bfloat16)

    def attend(g):
        query = queries[:, columns(g, 0)]
        keys = kv[:, columns(g, 0)]
        values = kv[:, columns(g, 1)]
        low = lax.broadcasted_iota(jnp.int32, (rows, PAIR), 1) < HEAD_DIM
        heads = []
        for head in range(2):
            chosen = low if head == 0 else jnp.logical_not(low)
            masked = jnp.where(chosen, query.astype(jnp.float32), 0.0).astype(jnp.bfloat16)
            scores = lax.dot_general(masked, keys, NT, preferred_element_type=jnp.float32)
            probs = jnp.exp(scores - jnp.max(scores, axis=-1, keepdims=True))
            totals = jnp.sum(probs, axis=-1, keepdims=True)
            summed = jnp.dot(
                probs.astype(jnp.bfloat16), values, preferred_element_type=jnp.float32
            )
            heads.append(summed / totals)
        attention[:, columns(g, 0)] = jnp.where(low, heads[0], heads[1]).astype(jnp.bfloat16)

    arrive(0)
    last = TILE // PAIR
    early = qw - TILE

    @pl.loop(0, pairs - last)
    def _(g):
        arrive(g + 1)
        ready(g)
        attend(g)

    for load in loads[6:]:
        load.wait()

    @pl.loop(0, width // TILE)
    def _(i):
        at = pl.ds(pl.multiple_of(i * TILE, TILE), TILE)
        tile = jnp.dot(
            attention[:, pl.ds(0, early)], wo[pl.ds(0, early), at],
            preferred_element_type=jnp.float32,
        )
        combined[:, at] = hidden[:, at].astype(jnp.float32) + gate[:, at] * tile

    for g in range(pairs - last, pairs):
        if g + 1 < pairs:
            arrive(g + 1)
        ready(g)
        attend(g)

    for i in range(width // TILE):
        at = pl.ds(i * TILE, TILE)
        tile = jnp.dot(
            attention[:, pl.ds(early, TILE)], wo[pl.ds(early, TILE), at],
            preferred_element_type=jnp.float32,
        )
        combined[:, at] += gate[:, at] * tile

    @pl.loop(0, rows // LN_ROWS)
    def _(i):
        at = pl.ds(pl.multiple_of(i * LN_ROWS, LN_ROWS), LN_ROWS)
        normed[at, :] = layer_norm(combined[at, :]).astype(jnp.bfloat16)

    velocity = lax.dot_general(wf[...], normed[...], NT, preferred_element_type=jnp.float32)
    advanced[...] = latent[...] + step_ref[0] * velocity

    seam = pltpu.make_async_remote_copy(
        src_ref=advanced,
        dst_ref=other,
        send_sem=seam_send,
        recv_sem=seam_recv,
        device_id=partner,
        device_id_type=MESH,
    )

    @pl.when(has_partner)
    def _():
        seam.start()

    @pl.loop(0, pairs)
    def _(g):
        for part in range(2):
            to_sibling(g, part).wait_send()
            for j in range(1, chips):
                to_peer(j, g, part).wait_send()
                forward(j, g, part).wait_send()

    @pl.when(has_partner)
    def _():
        seam_frames = half_devs * rows
        first = jnp.where(in_tail, f - half_devs, f) * rows
        place = first + lax.broadcasted_iota(jnp.int32, advanced.shape, 1)
        ramp = (place.astype(jnp.float32) + 0.5) / seam_frames
        own = jnp.where(in_tail, 1.0 - ramp, ramp)
        seam.wait()
        out_ref[...] = own * advanced[...] + (1.0 - own) * other[...]

    @pl.when(jnp.logical_not(has_partner))
    def _():
        out_ref[...] = advanced[...]


def on_device(
    windows,
    frame_devs,
    hidden_state,
    latent,
    stale_kv,
    mod_shift,
    mod_scale,
    mod_gate,
    w_query,
    w_keyval,
    w_out,
    w_final,
    step_size,
):
    rows, width = hidden_state.shape
    channels = latent.shape[1]
    qw = w_query.shape[1]
    pairs = qw // PAIR
    bf16, f32 = jnp.bfloat16, jnp.float32
    anywhere = pl.BlockSpec(memory_space=pl.ANY)
    result = pl.pallas_call(
        functools.partial(kernel, windows, frame_devs),
        out_shape=jax.ShapeDtypeStruct((channels, rows), f32),
        in_specs=[pl.BlockSpec(memory_space=pltpu.SMEM)] + [anywhere] * 10,
        out_specs=pl.BlockSpec(memory_space=pltpu.VMEM),
        scratch_shapes=[
            pltpu.VMEM((rows, width), bf16),
            pltpu.VMEM((channels, rows), f32),
            pltpu.VMEM((1, width), f32),
            pltpu.VMEM((1, width), f32),
            pltpu.VMEM((1, width), f32),
            pltpu.VMEM(w_query.shape, bf16),
            pltpu.VMEM(w_keyval.shape, bf16),
            pltpu.VMEM(w_out.shape, bf16),
            pltpu.VMEM((channels, width), bf16),
            pltpu.VMEM((rows, width), bf16),
            pltpu.VMEM((rows, qw), bf16),
            pltpu.VMEM((frame_devs * rows, 2 * qw), bf16),
            pltpu.VMEM((rows, qw), bf16),
            pltpu.VMEM((rows, width), f32),
            pltpu.VMEM((rows, width), bf16),
            pltpu.VMEM((channels, rows), f32),
            pltpu.VMEM((channels, rows), f32),
            pltpu.SemaphoreType.DMA((10,)),
            pltpu.SemaphoreType.DMA((frame_devs, pairs, 2)),
            pltpu.SemaphoreType.DMA((frame_devs, pairs, 2)),
            pltpu.SemaphoreType.DMA,
            pltpu.SemaphoreType.DMA,
        ],
        compiler_params=pltpu.CompilerParams(
            collective_id=0, has_side_effects=True, vmem_limit_bytes=56 * 1024 * 1024
        ),
        name="dit_window_step",
    )(
        step_size,
        hidden_state,
        latent.T,
        stale_kv,
        mod_shift,
        mod_scale,
        mod_gate,
        w_query,
        w_keyval,
        w_out,
        w_final.T,
    )
    return result.T


def solution(mesh):
    placed = (
        P(("win", "frm"), None),
        P(("win", "frm"), None),
        P(("win", "frm"), None),
        P("win", None),
        P("win", None),
        P("win", None),
        P(),
        P(),
        P(),
        P(),
        P("win"),
    )
    return jax.shard_map(
        functools.partial(on_device, mesh.shape["win"], mesh.shape["frm"]),
        mesh=mesh,
        in_specs=placed,
        out_specs=P(("win", "frm"), None),
        check_vma=False,
    )
```

```python
import functools

import jax
import jax.numpy as jnp
from jax import lax
from jax.experimental import pallas as pl
from jax.experimental.pallas import tpu as pltpu
from jax.sharding import PartitionSpec as P

HEAD_DIM = 64
PAIR = 2 * HEAD_DIM
TILE = 256
LN_ROWS = 32
MESH = pl.DeviceIdType.MESH
NT = (((1,), (1,)), ((), ()))


def layer_norm(values):
    average = jnp.mean(values, axis=-1, keepdims=True)
    centred = values - average
    variance = jnp.mean(centred * centred, axis=-1, keepdims=True)
    return centred * lax.rsqrt(variance + 1e-06)


def kernel(
    windows,
    frame_devs,
    step_hbm,
    hidden_hbm,
    latent_hbm,
    stale_hbm,
    shift_hbm,
    scale_hbm,
    gate_hbm,
    wq_hbm,
    wkv_hbm,
    wo_hbm,
    wf_hbm,
    advanced_hbm,
    other_hbm,
    step,
    hidden,
    latent,
    shift,
    scale,
    gate,
    wq,
    wkv,
    wo,
    wf,
    modulated,
    queries,
    kv,
    attention,
    maxima,
    totals,
    running,
    combined,
    normed,
    advanced,
    load_sem,
    send_sem,
    recv_sem,
    seam_send,
    seam_recv,
):
    rows, width = hidden.shape
    qw = queries.shape[1]
    pairs = qw // PAIR
    chips = frame_devs // 2
    half_devs = frame_devs // 2
    w = lax.axis_index("win")
    f = lax.axis_index("frm")
    chip, core = f // 2, f % 2
    sibling = (w, chip * 2 + (1 - core))
    peers = [(w, ((chip + j) % chips) * 2 + core) for j in range(1, chips)]
    in_tail = f >= half_devs
    has_partner = jnp.where(in_tail, w < windows - 1, w > 0)
    partner = (
        jnp.where(in_tail, w + 1, w - 1),
        jnp.where(in_tail, f - half_devs, f + half_devs),
    )

    loads = [
        pltpu.make_async_copy(src, dst, load_sem.at[i])
        for i, (src, dst) in enumerate(
            [
                (hidden_hbm, hidden),
                (scale_hbm, scale),
                (shift_hbm, shift),
                (wq_hbm, wq),
                (wkv_hbm.at[:, pl.ds(0, qw)], wkv.at[:, pl.ds(0, qw)]),
                (wkv_hbm.at[:, pl.ds(qw, qw)], wkv.at[:, pl.ds(qw, qw)]),
                (gate_hbm, gate),
                (wo_hbm, wo),
                (wf_hbm, wf),
                (latent_hbm, latent),
                (step_hbm, step),
            ]
        )
    ]
    for load in loads:
        load.start()

    barrier = pltpu.get_barrier_semaphore()
    for device in [sibling] + peers:
        pl.semaphore_signal(barrier, inc=1, device_id=device, device_id_type=MESH)

    @pl.when(has_partner)
    def _():
        pl.semaphore_signal(barrier, inc=1, device_id=partner, device_id_type=MESH)

    pl.semaphore_wait(barrier, jnp.where(has_partner, chips + 1, chips))

    def columns(g, part):
        return pl.ds(pl.multiple_of(part * qw + g * PAIR, PAIR), PAIR)

    def send(source, slot, device, g, part):
        return pltpu.make_async_remote_copy(
            src_ref=source.at[:, columns(g, part)],
            dst_ref=kv.at[pl.ds(slot * rows, rows), columns(g, part)],
            send_sem=send_sem.at[slot, g, part],
            recv_sem=recv_sem.at[slot, g, part],
            device_id=device,
            device_id_type=MESH,
        )

    def to_sibling(g, part):
        return send(stale_hbm, 1, sibling, g, part)

    def to_peer(j, g, part):
        return send(stale_hbm, 2 * j, peers[j - 1], g, part)

    def forward(j, g, part):
        return send(kv.at[pl.ds(2 * j * rows, rows)], 2 * j + 1, sibling, g, part)

    @pl.loop(0, pairs)
    def _(g):
        for part in range(2):
            for j in range(1, chips):
                to_peer(j, g, part).start()
            to_sibling(g, part).start()

    def arrive(g):
        for j in range(1, chips):
            for part in range(2):
                to_peer(j, g, part).wait_recv()
                forward(j, g, part).start()

    for load in loads[:3]:
        load.wait()

    @pl.loop(0, rows // LN_ROWS)
    def _(i):
        at = pl.ds(pl.multiple_of(i * LN_ROWS, LN_ROWS), LN_ROWS)
        line = layer_norm(hidden[at, :].astype(jnp.float32))
        modulated[at, :] = (line * (1.0 + scale[...]) + shift[...]).astype(jnp.bfloat16)

    loads[3].wait()

    @pl.loop(0, qw // TILE)
    def _(i):
        at = pl.ds(pl.multiple_of(i * TILE, TILE), TILE)
        tile = jnp.dot(modulated[...], wq[:, at], preferred_element_type=jnp.float32)
        queries[:, at] = (tile * HEAD_DIM ** (-0.5)).astype(jnp.bfloat16)

    loads[4].wait()
    loads[5].wait()

    @pl.loop(0, 2 * qw // TILE)
    def _(i):
        at = pl.ds(pl.multiple_of(i * TILE, TILE), TILE)
        tile = jnp.dot(modulated[...], wkv[:, at], preferred_element_type=jnp.float32)
        kv[pl.ds(0, rows), at] = tile.astype(jnp.bfloat16)

    low = lax.broadcasted_iota(jnp.int32, (rows, PAIR), 1) < HEAD_DIM

    def attend(g, slot, slots, first, final):
        at = columns(g, 0)
        held = pl.ds(slot * rows, slots * rows)
        query = queries[:, at].astype(jnp.float32)
        keys, values = kv[held, at], kv[held, columns(g, 1)]
        heads = []
        for chosen in (low, jnp.logical_not(low)):
            masked = jnp.where(chosen, query, 0.0).astype(jnp.bfloat16)
            scores = lax.dot_general(masked, keys, NT, preferred_element_type=jnp.float32)
            top = jnp.max(scores, axis=-1, keepdims=True)
            probs = jnp.exp(scores - top)
            total = jnp.sum(probs, axis=-1, keepdims=True)
            summed = jnp.dot(
                probs.astype(jnp.bfloat16), values, preferred_element_type=jnp.float32
            )
            heads.append((top, total, summed))
        top, total, summed = (jnp.where(low, *both) for both in zip(*heads))
        if not first:
            peak = jnp.maximum(maxima[:, at], top)
            keep, add = jnp.exp(maxima[:, at] - peak), jnp.exp(top - peak)
            top = peak
            total = totals[:, at] * keep + total * add
            summed = running[:, at] * keep + summed * add
        if final:
            attention[:, at] = (summed / total).astype(jnp.bfloat16)
        else:
            maxima[:, at], totals[:, at], running[:, at] = top, total, summed

    def attend_local(start, stop):
        @pl.loop(start, stop)
        def _(g):
            for part in range(2):
                to_sibling(g, part).wait_recv()
            attend(g, 0, 2, True, chips == 1)

    def attend_remote(g):
        for j in range(1, chips):
            attend(g, 2 * j, 1, False, False)
            for part in range(2):
                forward(j, g, part).wait_recv()
            attend(g, 2 * j + 1, 1, False, j == chips - 1)

    arrive(0)
    attend_local(0, pairs // 2)
    arrive(1)
    attend_local(pairs // 2, pairs)
    arrive(2)
    last = TILE // PAIR
    early = qw - TILE

    @pl.loop(0, 3)
    def _(g):
        attend_remote(g)

    @pl.loop(3, pairs - last)
    def _(g):
        arrive(g)
        attend_remote(g)

    for load in loads[6:]:
        load.wait()

    @pl.loop(0, width // TILE)
    def _(i):
        at = pl.ds(pl.multiple_of(i * TILE, TILE), TILE)
        tile = jnp.dot(
            attention[:, pl.ds(0, early)], wo[pl.ds(0, early), at],
            preferred_element_type=jnp.float32,
        )
        combined[:, at] = hidden[:, at].astype(jnp.float32) + gate[:, at] * tile

    @pl.loop(pairs - last, pairs)
    def _(g):
        arrive(g)
        attend_remote(g)

    for i in range(width // TILE):
        at = pl.ds(i * TILE, TILE)
        tile = jnp.dot(
            attention[:, pl.ds(early, TILE)], wo[pl.ds(early, TILE), at],
            preferred_element_type=jnp.float32,
        )
        combined[:, at] += gate[:, at] * tile

    @pl.loop(0, rows // LN_ROWS)
    def _(i):
        at = pl.ds(pl.multiple_of(i * LN_ROWS, LN_ROWS), LN_ROWS)
        normed[at, :] = layer_norm(combined[at, :]).astype(jnp.bfloat16)

    velocity = lax.dot_general(wf[...], normed[...], NT, preferred_element_type=jnp.float32)
    advanced[...] = latent[...] + step[0] * velocity

    keep = pltpu.make_async_copy(advanced, advanced_hbm, load_sem.at[len(loads)])
    seam = pltpu.make_async_remote_copy(
        src_ref=advanced,
        dst_ref=other_hbm,
        send_sem=seam_send,
        recv_sem=seam_recv,
        device_id=partner,
        device_id_type=MESH,
    )

    @pl.when(has_partner)
    def _():
        seam.start()

    keep.start()

    @pl.loop(0, pairs)
    def _(g):
        for part in range(2):
            to_sibling(g, part).wait_send()
            for j in range(1, chips):
                to_peer(j, g, part).wait_send()
                forward(j, g, part).wait_send()

    keep.wait()

    @pl.when(has_partner)
    def _():
        seam.wait()


def on_device(
    windows,
    frame_devs,
    hidden_state,
    latent,
    stale_kv,
    mod_shift,
    mod_scale,
    mod_gate,
    w_query,
    w_keyval,
    w_out,
    w_final,
    step_size,
):
    rows, width = hidden_state.shape
    channels = latent.shape[1]
    qw = w_query.shape[1]
    pairs = qw // PAIR
    bf16, f32 = jnp.bfloat16, jnp.float32
    anywhere = pl.BlockSpec(memory_space=pl.ANY)
    advanced, other = pl.pallas_call(
        functools.partial(kernel, windows, frame_devs),
        out_shape=[jax.ShapeDtypeStruct((channels, rows), f32)] * 2,
        in_specs=[pl.BlockSpec(memory_space=pltpu.HBM)] + [anywhere] * 10,
        out_specs=[anywhere] * 2,
        scratch_shapes=[
            pltpu.SMEM((1,), f32),
            pltpu.VMEM((rows, width), bf16),
            pltpu.VMEM((channels, rows), f32),
            pltpu.VMEM((1, width), f32),
            pltpu.VMEM((1, width), f32),
            pltpu.VMEM((1, width), f32),
            pltpu.VMEM(w_query.shape, bf16),
            pltpu.VMEM(w_keyval.shape, bf16),
            pltpu.VMEM(w_out.shape, bf16),
            pltpu.VMEM((channels, width), bf16),
            pltpu.VMEM((rows, width), bf16),
            pltpu.VMEM((rows, qw), bf16),
            pltpu.VMEM((frame_devs * rows, 2 * qw), bf16),
            pltpu.VMEM((rows, qw), bf16),
            pltpu.VMEM((rows, qw), f32),
            pltpu.VMEM((rows, qw), f32),
            pltpu.VMEM((rows, qw), f32),
            pltpu.VMEM((rows, width), f32),
            pltpu.VMEM((rows, width), bf16),
            pltpu.VMEM((channels, rows), f32),
            pltpu.SemaphoreType.DMA((12,)),
            pltpu.SemaphoreType.DMA((frame_devs, pairs, 2)),
            pltpu.SemaphoreType.DMA((frame_devs, pairs, 2)),
            pltpu.SemaphoreType.DMA,
            pltpu.SemaphoreType.DMA,
        ],
        compiler_params=pltpu.CompilerParams(
            collective_id=0, has_side_effects=True, vmem_limit_bytes=56 * 1024 * 1024
        ),
        name="dit_window_step",
    )(
        step_size,
        hidden_state,
        latent.T,
        stale_kv,
        mod_shift,
        mod_scale,
        mod_gate,
        w_query,
        w_keyval,
        w_out,
        w_final.T,
    )
    w, f = lax.axis_index("win"), lax.axis_index("frm")
    half_devs = frame_devs // 2
    in_tail = f >= half_devs
    has_partner = jnp.where(in_tail, w < windows - 1, w > 0)
    first = jnp.where(in_tail, f - half_devs, f) * rows
    place = first + lax.broadcasted_iota(jnp.int32, (channels, rows), 1)
    ramp = (place.astype(f32) + 0.5) / (half_devs * rows)
    own = jnp.where(in_tail, 1.0 - ramp, ramp)
    blended = jnp.where(has_partner, own * advanced + (1.0 - own) * other, advanced)
    return blended.T


def solution(mesh):
    placed = (
        P(("win", "frm"), None),
        P(("win", "frm"), None),
        P(("win", "frm"), None),
        P("win", None),
        P("win", None),
        P("win", None),
        P(),
        P(),
        P(),
        P(),
        P("win"),
    )
    return jax.shard_map(
        functools.partial(on_device, mesh.shape["win"], mesh.shape["frm"]),
        mesh=mesh,
        in_specs=placed,
        out_specs=P(("win", "frm"), None),
        check_vma=False,
    )
```

```python
import functools

import jax
import jax.numpy as jnp
from jax import lax
from jax.experimental import pallas as pl
from jax.experimental.pallas import tpu as pltpu
from jax.sharding import PartitionSpec as P

HEAD_DIM = 64
AHEAD = 3
PAIR = 2 * HEAD_DIM
TILE = 256
LN_ROWS = 32
MESH = pl.DeviceIdType.MESH
NT = (((1,), (1,)), ((), ()))


def layer_norm(values):
    average = jnp.mean(values, axis=-1, keepdims=True)
    centred = values - average
    variance = jnp.mean(centred * centred, axis=-1, keepdims=True)
    return centred * lax.rsqrt(variance + 1e-06)


def kernel(
    windows,
    frame_devs,
    step_hbm,
    hidden_hbm,
    latent_hbm,
    stale_hbm,
    shift_hbm,
    scale_hbm,
    gate_hbm,
    wq_hbm,
    wkv_hbm,
    wo_hbm,
    wf_hbm,
    advanced_hbm,
    other_hbm,
    step,
    hidden,
    latent,
    shift,
    scale,
    gate,
    wq,
    wkv,
    wo,
    wf,
    modulated,
    queries,
    own,
    kv,
    attention,
    maxima,
    totals,
    running,
    combined,
    normed,
    advanced,
    load_sem,
    stage_sem,
    send_sem,
    recv_sem,
    seam_send,
    seam_recv,
):
    rows, width = hidden.shape
    qw = queries.shape[1]
    pairs = qw // PAIR
    chips = frame_devs // 2
    half_devs = frame_devs // 2
    w = lax.axis_index("win")
    f = lax.axis_index("frm")
    chip, core = f // 2, f % 2
    sibling = (w, chip * 2 + (1 - core))
    peers = [(w, ((chip + j) % chips) * 2 + core) for j in range(1, chips)]
    in_tail = f >= half_devs
    has_partner = jnp.where(in_tail, w < windows - 1, w > 0)
    partner = (
        jnp.where(in_tail, w + 1, w - 1),
        jnp.where(in_tail, f - half_devs, f + half_devs),
    )

    loads = [
        pltpu.make_async_copy(src, dst, load_sem.at[i])
        for i, (src, dst) in enumerate(
            [
                (hidden_hbm, hidden),
                (scale_hbm, scale),
                (shift_hbm, shift),
                (wq_hbm, wq),
                (wkv_hbm.at[:, pl.ds(0, qw)], wkv.at[:, pl.ds(0, qw)]),
                (wkv_hbm.at[:, pl.ds(qw, qw)], wkv.at[:, pl.ds(qw, qw)]),
                (gate_hbm, gate),
                (wo_hbm, wo),
                (wf_hbm, wf),
                (latent_hbm, latent),
                (step_hbm, step),
            ]
        )
    ]
    def stage(g, part):
        at = pl.ds(pl.multiple_of(part * qw + g * PAIR, PAIR), PAIR)
        return pltpu.make_async_copy(
            stale_hbm.at[:, at], own.at[part * pairs + g], stage_sem.at[g, part]
        )

    @pl.loop(0, pairs)
    def _(g):
        for part in range(2):
            stage(g, part).start()

    for load in loads:
        load.start()

    barrier = pltpu.get_barrier_semaphore()
    for device in [sibling] + peers:
        pl.semaphore_signal(barrier, inc=1, device_id=device, device_id_type=MESH)

    @pl.when(has_partner)
    def _():
        pl.semaphore_signal(barrier, inc=1, device_id=partner, device_id_type=MESH)

    pl.semaphore_wait(barrier, jnp.where(has_partner, chips + 1, chips))

    def columns(g):
        return pl.ds(pl.multiple_of(g * PAIR, PAIR), PAIR)

    def send(source, slot, device, g, part):
        return pltpu.make_async_remote_copy(
            src_ref=source,
            dst_ref=kv.at[part * pairs + g, pl.ds(slot * rows, rows)],
            send_sem=send_sem.at[slot, g, part],
            recv_sem=recv_sem.at[slot, g, part],
            device_id=device,
            device_id_type=MESH,
        )

    def to_sibling(g, part):
        return send(own.at[part * pairs + g], 1, sibling, g, part)

    def to_peer(j, g, part):
        return send(own.at[part * pairs + g], 2 * j, peers[j - 1], g, part)

    def forward(j, g, part):
        source = kv.at[part * pairs + g, pl.ds(2 * j * rows, rows)]
        return send(source, 2 * j + 1, sibling, g, part)

    def launch(g):
        for part in range(2):
            for j in range(1, chips):
                to_peer(j, g, part).start()

    def arrive(g):
        for j in range(1, chips):
            for part in range(2):
                to_peer(j, g, part).wait_recv()
                forward(j, g, part).start()

    @pl.loop(0, AHEAD)
    def _(g):
        for part in range(2):
            stage(g, part).wait()
        launch(g)
        for part in range(2):
            to_sibling(g, part).start()

    def advance(g):
        arrive(g)
        for part in range(2):
            for j in range(1, chips):
                to_peer(j, g, part).wait_send()
        if isinstance(g, int):
            if g + AHEAD < pairs:
                launch(g + AHEAD)
        else:
            @pl.when(g + AHEAD < pairs)
            def _():
                launch(g + AHEAD)

    @pl.loop(AHEAD, pairs)
    def _(g):
        for part in range(2):
            stage(g, part).wait()
            to_sibling(g, part).start()

    for load in loads[:3]:
        load.wait()

    @pl.loop(0, rows // LN_ROWS)
    def _(i):
        at = pl.ds(pl.multiple_of(i * LN_ROWS, LN_ROWS), LN_ROWS)
        line = layer_norm(hidden[at, :].astype(jnp.float32))
        modulated[at, :] = (line * (1.0 + scale[...]) + shift[...]).astype(jnp.bfloat16)

    loads[3].wait()

    @pl.loop(0, qw // TILE)
    def _(i):
        at = pl.ds(pl.multiple_of(i * TILE, TILE), TILE)
        tile = jnp.dot(modulated[...], wq[:, at], preferred_element_type=jnp.float32)
        queries[:, at] = (tile * HEAD_DIM ** (-0.5)).astype(jnp.bfloat16)

    loads[4].wait()
    loads[5].wait()

    @pl.loop(0, 2 * qw // TILE)
    def _(i):
        at = pl.ds(pl.multiple_of(i * TILE, TILE), TILE)
        tile = jnp.dot(modulated[...], wkv[:, at], preferred_element_type=jnp.float32)
        for k in range(TILE // PAIR):
            piece = tile[:, k * PAIR : (k + 1) * PAIR].astype(jnp.bfloat16)
            kv[(TILE // PAIR) * i + k, pl.ds(0, rows)] = piece

    low = lax.broadcasted_iota(jnp.int32, (rows, PAIR), 1) < HEAD_DIM

    def attend(g, slot, slots, first, final):
        at = columns(g)
        held = pl.ds(slot * rows, slots * rows)
        query = queries[:, at].astype(jnp.float32)
        keys, values = kv[g, held], kv[pairs + g, held]
        heads = []
        for chosen in (low, jnp.logical_not(low)):
            masked = jnp.where(chosen, query, 0.0).astype(jnp.bfloat16)
            scores = lax.dot_general(masked, keys, NT, preferred_element_type=jnp.float32)
            top = jnp.max(scores, axis=-1, keepdims=True)
            probs = jnp.exp(scores - top)
            total = jnp.sum(probs, axis=-1, keepdims=True)
            summed = jnp.dot(
                probs.astype(jnp.bfloat16), values, preferred_element_type=jnp.float32
            )
            heads.append((top, total, summed))
        top, total, summed = (jnp.where(low, *both) for both in zip(*heads))
        if not first:
            peak = jnp.maximum(maxima[:, at], top)
            keep, add = jnp.exp(maxima[:, at] - peak), jnp.exp(top - peak)
            top = peak
            total = totals[:, at] * keep + total * add
            summed = running[:, at] * keep + summed * add
        if final:
            attention[:, at] = (summed / total).astype(jnp.bfloat16)
        else:
            maxima[:, at], totals[:, at], running[:, at] = top, total, summed

    def attend_local(start, stop):
        @pl.loop(start, stop)
        def _(g):
            for part in range(2):
                to_sibling(g, part).wait_recv()
            attend(g, 0, 2, True, chips == 1)

    def attend_remote(g):
        for j in range(1, chips):
            attend(g, 2 * j, 1, False, False)
            for part in range(2):
                forward(j, g, part).wait_recv()
            attend(g, 2 * j + 1, 1, False, j == chips - 1)

    advance(0)
    attend_local(0, pairs // 2)
    advance(1)
    attend_local(pairs // 2, pairs)
    advance(2)
    last = TILE // PAIR
    early = qw - TILE

    @pl.loop(0, 3)
    def _(g):
        attend_remote(g)

    @pl.loop(3, pairs - last)
    def _(g):
        advance(g)
        attend_remote(g)

    for load in loads[6:]:
        load.wait()

    @pl.loop(0, width // TILE)
    def _(i):
        at = pl.ds(pl.multiple_of(i * TILE, TILE), TILE)
        tile = jnp.dot(
            attention[:, pl.ds(0, early)], wo[pl.ds(0, early), at],
            preferred_element_type=jnp.float32,
        )
        combined[:, at] = hidden[:, at].astype(jnp.float32) + gate[:, at] * tile

    @pl.loop(pairs - last, pairs)
    def _(g):
        advance(g)
        attend_remote(g)

    for i in range(width // TILE):
        at = pl.ds(i * TILE, TILE)
        tile = jnp.dot(
            attention[:, pl.ds(early, TILE)], wo[pl.ds(early, TILE), at],
            preferred_element_type=jnp.float32,
        )
        combined[:, at] += gate[:, at] * tile

    @pl.loop(0, rows // LN_ROWS)
    def _(i):
        at = pl.ds(pl.multiple_of(i * LN_ROWS, LN_ROWS), LN_ROWS)
        normed[at, :] = layer_norm(combined[at, :]).astype(jnp.bfloat16)

    velocity = lax.dot_general(wf[...], normed[...], NT, preferred_element_type=jnp.float32)
    advanced[...] = latent[...] + step[0] * velocity

    keep = pltpu.make_async_copy(advanced, advanced_hbm, load_sem.at[len(loads)])
    seam = pltpu.make_async_remote_copy(
        src_ref=advanced,
        dst_ref=other_hbm,
        send_sem=seam_send,
        recv_sem=seam_recv,
        device_id=partner,
        device_id_type=MESH,
    )

    @pl.when(has_partner)
    def _():
        seam.start()

    keep.start()

    @pl.loop(0, pairs)
    def _(g):
        for part in range(2):
            to_sibling(g, part).wait_send()
            for j in range(1, chips):
                forward(j, g, part).wait_send()

    keep.wait()

    @pl.when(has_partner)
    def _():
        seam.wait()


def on_device(
    windows,
    frame_devs,
    hidden_state,
    latent,
    stale_kv,
    mod_shift,
    mod_scale,
    mod_gate,
    w_query,
    w_keyval,
    w_out,
    w_final,
    step_size,
):
    rows, width = hidden_state.shape
    channels = latent.shape[1]
    qw = w_query.shape[1]
    pairs = qw // PAIR
    bf16, f32 = jnp.bfloat16, jnp.float32
    anywhere = pl.BlockSpec(memory_space=pl.ANY)
    advanced, other = pl.pallas_call(
        functools.partial(kernel, windows, frame_devs),
        out_shape=[jax.ShapeDtypeStruct((channels, rows), f32)] * 2,
        in_specs=[anywhere] + [pl.BlockSpec(memory_space=pltpu.HBM)] * 10,
        out_specs=[anywhere] * 2,
        scratch_shapes=[
            pltpu.SMEM((1,), f32),
            pltpu.VMEM((rows, width), bf16),
            pltpu.VMEM((channels, rows), f32),
            pltpu.VMEM((1, width), f32),
            pltpu.VMEM((1, width), f32),
            pltpu.VMEM((1, width), f32),
            pltpu.VMEM(w_query.shape, bf16),
            pltpu.VMEM(w_keyval.shape, bf16),
            pltpu.VMEM(w_out.shape, bf16),
            pltpu.VMEM((channels, width), bf16),
            pltpu.VMEM((rows, width), bf16),
            pltpu.VMEM((rows, qw), bf16),
            pltpu.VMEM((2 * pairs, rows, PAIR), bf16),
            pltpu.VMEM((2 * pairs, frame_devs * rows, PAIR), bf16),
            pltpu.VMEM((rows, qw), bf16),
            pltpu.VMEM((rows, qw), f32),
            pltpu.VMEM((rows, qw), f32),
            pltpu.VMEM((rows, qw), f32),
            pltpu.VMEM((rows, width), f32),
            pltpu.VMEM((rows, width), bf16),
            pltpu.VMEM((channels, rows), f32),
            pltpu.SemaphoreType.DMA((12,)),
            pltpu.SemaphoreType.DMA((pairs, 2)),
            pltpu.SemaphoreType.DMA((frame_devs, pairs, 2)),
            pltpu.SemaphoreType.DMA((frame_devs, pairs, 2)),
            pltpu.SemaphoreType.DMA,
            pltpu.SemaphoreType.DMA,
        ],
        compiler_params=pltpu.CompilerParams(
            collective_id=0, has_side_effects=True, vmem_limit_bytes=44 * 1024 * 1024
        ),
        name="dit_window_step",
    )(
        step_size,
        *(
            pltpu.with_memory_space_constraint(operand, pltpu.HBM)
            for operand in (
                hidden_state,
                latent.T,
                stale_kv,
                mod_shift,
                mod_scale,
                mod_gate,
                w_query,
                w_keyval,
                w_out,
                w_final.T,
            )
        )
    )
    w, f = lax.axis_index("win"), lax.axis_index("frm")
    half_devs = frame_devs // 2
    in_tail = f >= half_devs
    has_partner = jnp.where(in_tail, w < windows - 1, w > 0)
    first = jnp.where(in_tail, f - half_devs, f) * rows
    place = first + lax.broadcasted_iota(jnp.int32, (channels, rows), 1)
    ramp = (place.astype(f32) + 0.5) / (half_devs * rows)
    own = jnp.where(in_tail, 1.0 - ramp, ramp)
    blended = jnp.where(has_partner, own * advanced + (1.0 - own) * other, advanced)
    return blended.T


def solution(mesh):
    placed = (
        P(("win", "frm"), None),
        P(("win", "frm"), None),
        P(("win", "frm"), None),
        P("win", None),
        P("win", None),
        P("win", None),
        P(),
        P(),
        P(),
        P(),
        P("win"),
    )
    return jax.shard_map(
        functools.partial(on_device, mesh.shape["win"], mesh.shape["frm"]),
        mesh=mesh,
        in_specs=placed,
        out_specs=P(("win", "frm"), None),
        check_vma=False,
    )
```

```python
import functools

import jax
import jax.numpy as jnp
from jax import lax
from jax.experimental import pallas as pl
from jax.experimental.pallas import tpu as pltpu
from jax.sharding import PartitionSpec as P

HEAD_DIM = 64
AHEAD = 3
PAIR = 2 * HEAD_DIM
TILE = 256
LN_ROWS = 64
MESH = pl.DeviceIdType.MESH


def layer_norm(values):
    average = jnp.mean(values, axis=-1, keepdims=True)
    centred = values - average
    variance = jnp.mean(centred * centred, axis=-1, keepdims=True)
    return centred * lax.rsqrt(variance + 1e-06)


def flip(block):
    return block.astype(jnp.float32).T.astype(block.dtype)


def kernel(
    windows,
    frame_devs,
    step_hbm,
    hidden_hbm,
    latent_hbm,
    stale_hbm,
    shift_hbm,
    scale_hbm,
    gate_hbm,
    wq_hbm,
    wkv_hbm,
    wo_hbm,
    wf_hbm,
    advanced_hbm,
    other_hbm,
    step,
    hidden,
    latent,
    shift,
    scale,
    gate,
    wq,
    wkv,
    wo,
    wf,
    wf_rows,
    modulated,
    queries,
    staged,
    own,
    keys,
    values,
    attention,
    maxima,
    totals,
    running,
    combined,
    normed,
    advanced,
    load_sem,
    stage_sem,
    send_sem,
    recv_sem,
    seam_send,
    seam_recv,
):
    rows, width = hidden.shape
    qw = wq.shape[1]
    pairs = qw // PAIR
    chips = frame_devs // 2
    half_devs = frame_devs // 2
    w = lax.axis_index("win")
    f = lax.axis_index("frm")
    chip, core = f // 2, f % 2
    sibling = (w, chip * 2 + (1 - core))
    peers = [(w, ((chip + j) % chips) * 2 + core) for j in range(1, chips)]
    in_tail = f >= half_devs
    has_partner = jnp.where(in_tail, w < windows - 1, w > 0)
    partner = (
        jnp.where(in_tail, w + 1, w - 1),
        jnp.where(in_tail, f - half_devs, f + half_devs),
    )

    loads = [
        pltpu.make_async_copy(src, dst, load_sem.at[i])
        for i, (src, dst) in enumerate(
            [
                (hidden_hbm, hidden),
                (scale_hbm, scale),
                (shift_hbm, shift),
                (wq_hbm, wq),
                (wkv_hbm.at[:, pl.ds(0, qw)], wkv.at[:, pl.ds(0, qw)]),
                (wkv_hbm.at[:, pl.ds(qw, qw)], wkv.at[:, pl.ds(qw, qw)]),
                (gate_hbm, gate),
                (wo_hbm, wo),
                (wf_hbm, wf),
                (latent_hbm, latent),
                (step_hbm, step),
            ]
        )
    ]
    def stage(g, part):
        at = pl.ds(pl.multiple_of(part * qw + g * PAIR, PAIR), PAIR)
        return pltpu.make_async_copy(
            stale_hbm.at[:, at], staged.at[part * pairs + g], stage_sem.at[g, part]
        )

    @pl.loop(0, pairs)
    def _(g):
        for part in range(2):
            stage(g, part).start()

    for load in loads:
        load.start()

    barrier = pltpu.get_barrier_semaphore()
    for device in [sibling] + peers:
        pl.semaphore_signal(barrier, inc=1, device_id=device, device_id_type=MESH)

    @pl.when(has_partner)
    def _():
        pl.semaphore_signal(barrier, inc=1, device_id=partner, device_id_type=MESH)

    pl.semaphore_wait(barrier, jnp.where(has_partner, chips + 1, chips))

    def columns(g):
        return pl.ds(pl.multiple_of(g * PAIR, PAIR), PAIR)

    def place(slot, g, part):
        return values.at[g, slot] if part else keys.at[g, pl.ds(slot * rows, rows)]

    def source(g, part):
        return own.at[g] if part else staged.at[g]

    def send(ref, slot, device, g, part):
        return pltpu.make_async_remote_copy(
            src_ref=ref,
            dst_ref=place(slot, g, part),
            send_sem=send_sem.at[slot, g, part],
            recv_sem=recv_sem.at[slot, g, part],
            device_id=device,
            device_id_type=MESH,
        )

    def to_sibling(g, part):
        return send(source(g, part), 1, sibling, g, part)

    def to_peer(j, g, part):
        return send(source(g, part), 2 * j, peers[j - 1], g, part)

    def forward(j, g, part):
        return send(place(2 * j, g, part), 2 * j + 1, sibling, g, part)

    def launch(g, part):
        for j in range(1, chips):
            to_peer(j, g, part).start()

    def arrive(g):
        for j in range(1, chips):
            for part in range(2):
                to_peer(j, g, part).wait_recv()
                forward(j, g, part).start()

    @pl.loop(0, pairs)
    def _(g):
        for part in range(2):
            stage(g, part).wait()
            if part:
                own[g] = flip(staged[pairs + g])

            @pl.when(g < AHEAD)
            def _():
                launch(g, part)

            to_sibling(g, part).start()

    def advance(g):
        arrive(g)
        for part in range(2):
            for j in range(1, chips):
                to_peer(j, g, part).wait_send()

        @pl.when(g + AHEAD < pairs)
        def _():
            for part in range(2):
                launch(g + AHEAD, part)

    for load in loads[:3]:
        load.wait()

    for start in range(0, rows, LN_ROWS):
        at = pl.ds(start, LN_ROWS)
        line = layer_norm(hidden[at, :].astype(jnp.float32))
        modulated[at, :] = (line * (1.0 + scale[...]) + shift[...]).astype(jnp.bfloat16)

    loads[3].wait()
    blank = jnp.zeros((HEAD_DIM, rows), jnp.bfloat16)

    @pl.loop(0, qw // TILE)
    def _(i):
        at = pl.ds(pl.multiple_of(i * TILE, TILE), TILE)
        tile = jnp.dot(modulated[...], wq[:, at], preferred_element_type=jnp.float32)
        tile = (tile * HEAD_DIM ** (-0.5)).T.astype(jnp.bfloat16)
        for k in range(TILE // PAIR):
            g = (TILE // PAIR) * i + k
            first, second = k * PAIR, k * PAIR + HEAD_DIM
            queries[g, 0:HEAD_DIM, 0:rows] = tile[first:second]
            queries[g, HEAD_DIM:PAIR, 0:rows] = blank
            queries[g, 0:HEAD_DIM, rows : 2 * rows] = blank
            queries[g, HEAD_DIM:PAIR, rows : 2 * rows] = tile[second : second + HEAD_DIM]

    loads[4].wait()

    @pl.loop(0, qw // TILE)
    def _(i):
        at = pl.ds(pl.multiple_of(i * TILE, TILE), TILE)
        tile = jnp.dot(modulated[...], wkv[:, at], preferred_element_type=jnp.float32)
        for k in range(TILE // PAIR):
            piece = tile[:, k * PAIR : (k + 1) * PAIR].astype(jnp.bfloat16)
            keys[(TILE // PAIR) * i + k, 0:rows] = piece

    loads[5].wait()

    @pl.loop(0, qw // TILE)
    def _(i):
        at = pl.ds(pl.multiple_of(qw + i * TILE, TILE), TILE)
        tile = jnp.dot(modulated[...], wkv[:, at], preferred_element_type=jnp.float32)
        tile = tile.T.astype(jnp.bfloat16)
        for k in range(TILE // PAIR):
            values[(TILE // PAIR) * i + k, 0] = tile[k * PAIR : (k + 1) * PAIR]

    def attend(g, slot, slots, first, final):
        scores = jnp.dot(
            keys[g, pl.ds(slot * rows, slots * rows)], queries[g],
            preferred_element_type=jnp.float32,
        )
        top = jnp.max(scores, axis=0, keepdims=True)
        if not first:
            top = jnp.maximum(maxima[g], top)
        probs = jnp.exp(scores - top)
        total = jnp.sum(probs, axis=0, keepdims=True)
        if not first:
            kept = jnp.exp(maxima[g] - top)
            total = totals[g] * kept + total
        weights = probs.astype(jnp.bfloat16)
        heads = []
        for head in range(2):
            lanes = slice(head * rows, (head + 1) * rows)
            span = slice(head * HEAD_DIM, (head + 1) * HEAD_DIM)
            summed = running[g, span] * kept[:, lanes] if not first else None
            for k in range(slots):
                share = jnp.dot(
                    values[g, slot + k, span], weights[k * rows : (k + 1) * rows, lanes],
                    preferred_element_type=jnp.float32,
                )
                summed = share if summed is None else summed + share
            heads.append(summed / total[:, lanes] if final else summed)
        both = jnp.concatenate(heads, axis=0)
        if final:
            attention[:, columns(g)] = both.T.astype(jnp.bfloat16)
        else:
            maxima[g], totals[g], running[g] = top, total, both

    def attend_local(start, stop):
        @pl.loop(start, stop)
        def _(g):
            for part in range(2):
                to_sibling(g, part).wait_recv()
            attend(g, 0, 2, True, chips == 1)

    def attend_remote(g, together):
        for j in range(1, chips):
            if not together:
                attend(g, 2 * j, 1, False, False)
            for part in range(2):
                forward(j, g, part).wait_recv()
            if together:
                attend(g, 2 * j, 2, False, j == chips - 1)
            else:
                attend(g, 2 * j + 1, 1, False, j == chips - 1)

    advance(0)
    attend_local(0, pairs // 2)
    advance(1)
    attend_local(pairs // 2, pairs)
    advance(2)
    last = TILE // PAIR
    early = qw - TILE

    @pl.loop(0, 3)
    def _(g):
        attend_remote(g, True)

    @pl.loop(3, pairs - last)
    def _(g):
        advance(g)
        attend_remote(g, False)

    for load in loads[6:]:
        load.wait()
    wf_rows[...] = flip(wf[...])

    @pl.loop(0, width // TILE)
    def _(i):
        at = pl.ds(pl.multiple_of(i * TILE, TILE), TILE)
        tile = jnp.dot(
            attention[:, pl.ds(0, early)], wo[pl.ds(0, early), at],
            preferred_element_type=jnp.float32,
        )
        combined[:, at] = hidden[:, at].astype(jnp.float32) + gate[:, at] * tile

    @pl.loop(pairs - last, pairs)
    def _(g):
        advance(g)
        attend_remote(g, False)

    for i in range(width // TILE):
        at = pl.ds(i * TILE, TILE)
        tile = jnp.dot(
            attention[:, pl.ds(early, TILE)], wo[pl.ds(early, TILE), at],
            preferred_element_type=jnp.float32,
        )
        combined[:, at] += gate[:, at] * tile

    for start in range(0, rows, LN_ROWS):
        at = pl.ds(start, LN_ROWS)
        normed[at, :] = layer_norm(combined[at, :]).astype(jnp.bfloat16)

    velocity = jnp.dot(normed[...], wf_rows[...], preferred_element_type=jnp.float32)
    advanced[...] = latent[...] + step[0] * velocity.T

    keep = pltpu.make_async_copy(advanced, advanced_hbm, load_sem.at[len(loads)])
    seam = pltpu.make_async_remote_copy(
        src_ref=advanced,
        dst_ref=other_hbm,
        send_sem=seam_send,
        recv_sem=seam_recv,
        device_id=partner,
        device_id_type=MESH,
    )

    @pl.when(has_partner)
    def _():
        seam.start()

    keep.start()

    @pl.loop(0, pairs)
    def _(g):
        for part in range(2):
            to_sibling(g, part).wait_send()
            for j in range(1, chips):
                forward(j, g, part).wait_send()

    keep.wait()

    @pl.when(has_partner)
    def _():
        seam.wait()


def on_device(
    windows,
    frame_devs,
    hidden_state,
    latent,
    stale_kv,
    mod_shift,
    mod_scale,
    mod_gate,
    w_query,
    w_keyval,
    w_out,
    w_final,
    step_size,
):
    rows, width = hidden_state.shape
    channels = latent.shape[1]
    qw = w_query.shape[1]
    pairs = qw // PAIR
    bf16, f32 = jnp.bfloat16, jnp.float32
    anywhere = pl.BlockSpec(memory_space=pl.ANY)
    advanced, other = pl.pallas_call(
        functools.partial(kernel, windows, frame_devs),
        out_shape=[jax.ShapeDtypeStruct((channels, rows), f32)] * 2,
        in_specs=[anywhere] + [pl.BlockSpec(memory_space=pltpu.HBM)] * 10,
        out_specs=[anywhere] * 2,
        scratch_shapes=[
            pltpu.SMEM((1,), f32),
            pltpu.VMEM((rows, width), bf16),
            pltpu.VMEM((channels, rows), f32),
            pltpu.VMEM((1, width), f32),
            pltpu.VMEM((1, width), f32),
            pltpu.VMEM((1, width), f32),
            pltpu.VMEM(w_query.shape, bf16),
            pltpu.VMEM(w_keyval.shape, bf16),
            pltpu.VMEM(w_out.shape, bf16),
            pltpu.VMEM((channels, width), bf16),
            pltpu.VMEM((width, channels), bf16),
            pltpu.VMEM((rows, width), bf16),
            pltpu.VMEM((pairs, PAIR, 2 * rows), bf16),
            pltpu.VMEM((2 * pairs, rows, PAIR), bf16),
            pltpu.VMEM((pairs, PAIR, rows), bf16),
            pltpu.VMEM((pairs, frame_devs * rows, PAIR), bf16),
            pltpu.VMEM((pairs, frame_devs, PAIR, rows), bf16),
            pltpu.VMEM((rows, qw), bf16),
            pltpu.VMEM((pairs, 1, 2 * rows), f32),
            pltpu.VMEM((pairs, 1, 2 * rows), f32),
            pltpu.VMEM((pairs, PAIR, rows), f32),
            pltpu.VMEM((rows, width), f32),
            pltpu.VMEM((rows, width), bf16),
            pltpu.VMEM((channels, rows), f32),
            pltpu.SemaphoreType.DMA((12,)),
            pltpu.SemaphoreType.DMA((pairs, 2)),
            pltpu.SemaphoreType.DMA((frame_devs, pairs, 2)),
            pltpu.SemaphoreType.DMA((frame_devs, pairs, 2)),
            pltpu.SemaphoreType.DMA,
            pltpu.SemaphoreType.DMA,
        ],
        compiler_params=pltpu.CompilerParams(
            collective_id=0, has_side_effects=True, vmem_limit_bytes=44 * 1024 * 1024
        ),
        name="dit_window_step",
    )(
        step_size,
        *(
            pltpu.with_memory_space_constraint(operand, pltpu.HBM)
            for operand in (
                hidden_state,
                latent.T,
                stale_kv,
                mod_shift,
                mod_scale,
                mod_gate,
                w_query,
                w_keyval,
                w_out,
                w_final.T,
            )
        )
    )
    w, f = lax.axis_index("win"), lax.axis_index("frm")
    half_devs = frame_devs // 2
    in_tail = f >= half_devs
    has_partner = jnp.where(in_tail, w < windows - 1, w > 0)
    first = jnp.where(in_tail, f - half_devs, f) * rows
    place = first + lax.broadcasted_iota(jnp.int32, (channels, rows), 1)
    ramp = (place.astype(f32) + 0.5) / (half_devs * rows)
    own = jnp.where(in_tail, 1.0 - ramp, ramp)
    blended = jnp.where(has_partner, own * advanced + (1.0 - own) * other, advanced)
    return blended.T


def solution(mesh):
    placed = (
        P(("win", "frm"), None),
        P(("win", "frm"), None),
        P(("win", "frm"), None),
        P("win", None),
        P("win", None),
        P("win", None),
        P(),
        P(),
        P(),
        P(),
        P("win"),
    )
    return jax.shard_map(
        functools.partial(on_device, mesh.shape["win"], mesh.shape["frm"]),
        mesh=mesh,
        in_specs=placed,
        out_specs=P(("win", "frm"), None),
        check_vma=False,
    )
```

```python
import functools

import jax
import jax.numpy as jnp
from jax import lax
from jax.experimental import pallas as pl
from jax.experimental.pallas import tpu as pltpu
from jax.sharding import PartitionSpec as P

HEAD_DIM = 64
AHEAD = 4
PAIR = 2 * HEAD_DIM
TILE = 256
LN_ROWS = 64
MESH = pl.DeviceIdType.MESH


def layer_norm(values):
    average = jnp.mean(values, axis=-1, keepdims=True)
    centred = values - average
    variance = jnp.mean(centred * centred, axis=-1, keepdims=True)
    return centred * lax.rsqrt(variance + 1e-06)


def flip(block):
    return block.astype(jnp.float32).T.astype(block.dtype)


def kernel(
    windows,
    frame_devs,
    step_hbm,
    hidden_hbm,
    latent_hbm,
    stale_hbm,
    shift_hbm,
    scale_hbm,
    gate_hbm,
    wq_hbm,
    wkv_hbm,
    wo_hbm,
    wf_hbm,
    advanced_hbm,
    other_hbm,
    step,
    hidden,
    latent,
    shift,
    scale,
    gate,
    wq,
    wkv,
    wo,
    wf,
    wf_rows,
    modulated,
    queries,
    staged,
    own,
    keys,
    values,
    attention,
    maxima,
    totals,
    running,
    combined,
    normed,
    advanced,
    sent,
    load_sem,
    stage_sem,
    send_sem,
    recv_sem,
    seam_send,
    seam_recv,
):
    rows, width = hidden.shape
    qw = wq.shape[1]
    pairs = qw // PAIR
    chips = frame_devs // 2
    half_devs = frame_devs // 2
    w = lax.axis_index("win")
    f = lax.axis_index("frm")
    chip, core = f // 2, f % 2
    sibling = (w, chip * 2 + (1 - core))
    peers = [(w, ((chip + j) % chips) * 2 + core) for j in range(1, chips)]
    in_tail = f >= half_devs
    has_partner = jnp.where(in_tail, w < windows - 1, w > 0)
    partner = (
        jnp.where(in_tail, w + 1, w - 1),
        jnp.where(in_tail, f - half_devs, f + half_devs),
    )

    loads = [
        pltpu.make_async_copy(src, dst, load_sem.at[i])
        for i, (src, dst) in enumerate(
            [
                (hidden_hbm, hidden),
                (scale_hbm, scale),
                (shift_hbm, shift),
                (wq_hbm, wq),
                (wkv_hbm.at[:, pl.ds(0, qw)], wkv.at[:, pl.ds(0, qw)]),
                (wkv_hbm.at[:, pl.ds(qw, qw)], wkv.at[:, pl.ds(qw, qw)]),
                (gate_hbm, gate),
                (wo_hbm, wo),
                (wf_hbm, wf),
                (latent_hbm, latent),
                (step_hbm, step),
            ]
        )
    ]
    def stage(g, part):
        at = pl.ds(pl.multiple_of(part * qw + g * PAIR, PAIR), PAIR)
        return pltpu.make_async_copy(
            stale_hbm.at[:, at], staged.at[part * pairs + g], stage_sem.at[g, part]
        )

    @pl.loop(0, pairs)
    def _(g):
        for part in range(2):
            stage(g, part).start()

    for load in loads:
        load.start()

    barrier = pltpu.get_barrier_semaphore()
    for device in [sibling] + peers:
        pl.semaphore_signal(barrier, inc=1, device_id=device, device_id_type=MESH)

    @pl.when(has_partner)
    def _():
        pl.semaphore_signal(barrier, inc=1, device_id=partner, device_id_type=MESH)

    pl.semaphore_wait(barrier, jnp.where(has_partner, chips + 1, chips))

    def columns(g):
        return pl.ds(pl.multiple_of(g * PAIR, PAIR), PAIR)

    def place(slot, g, part):
        return values.at[g, slot] if part else keys.at[g, pl.ds(slot * rows, rows)]

    def source(g, part):
        return own.at[g] if part else staged.at[g]

    def send(ref, slot, device, g, part):
        return pltpu.make_async_remote_copy(
            src_ref=ref,
            dst_ref=place(slot, g, part),
            send_sem=send_sem.at[slot, g, part],
            recv_sem=recv_sem.at[slot, g, part],
            device_id=device,
            device_id_type=MESH,
        )

    def to_sibling(g, part):
        return send(source(g, part), 1, sibling, g, part)

    def to_peer(j, g, part):
        return send(source(g, part), 2 * j, peers[j - 1], g, part)

    def forward(j, g, part):
        return send(place(2 * j, g, part), 2 * j + 1, sibling, g, part)

    def launch(g, part):
        for j in range(1, chips):
            to_peer(j, g, part).start()

    def arrive(g):
        for j in range(1, chips):
            for part in range(2):
                to_peer(j, g, part).wait_recv()
                forward(j, g, part).start()

    @pl.loop(0, pairs)
    def _(g):
        for part in range(2):
            stage(g, part).wait()
            if part:
                own[g] = flip(staged[pairs + g])

            @pl.when(g < AHEAD)
            def _():
                launch(g, part)

            to_sibling(g, part).start()

    def advance(g):
        arrive(g)
        for part in range(2):
            for j in range(1, chips):
                to_peer(j, g, part).wait_send()

        @pl.when(g + AHEAD < pairs)
        def _():
            for part in range(2):
                launch(g + AHEAD, part)

    for load in loads[:3]:
        load.wait()

    for start in range(0, rows, LN_ROWS):
        at = pl.ds(start, LN_ROWS)
        line = layer_norm(hidden[at, :].astype(jnp.float32))
        modulated[at, :] = (line * (1.0 + scale[...]) + shift[...]).astype(jnp.bfloat16)

    loads[3].wait()
    blank = jnp.zeros((HEAD_DIM, rows), jnp.bfloat16)

    @pl.loop(0, qw // TILE)
    def _(i):
        at = pl.ds(pl.multiple_of(i * TILE, TILE), TILE)
        tile = jnp.dot(modulated[...], wq[:, at], preferred_element_type=jnp.float32)
        tile = (tile * HEAD_DIM ** (-0.5)).T.astype(jnp.bfloat16)
        for k in range(TILE // PAIR):
            g = (TILE // PAIR) * i + k
            first, second = k * PAIR, k * PAIR + HEAD_DIM
            queries[g, 0:HEAD_DIM, 0:rows] = tile[first:second]
            queries[g, HEAD_DIM:PAIR, 0:rows] = blank
            queries[g, 0:HEAD_DIM, rows : 2 * rows] = blank
            queries[g, HEAD_DIM:PAIR, rows : 2 * rows] = tile[second : second + HEAD_DIM]

    loads[4].wait()

    @pl.loop(0, qw // TILE)
    def _(i):
        at = pl.ds(pl.multiple_of(i * TILE, TILE), TILE)
        tile = jnp.dot(modulated[...], wkv[:, at], preferred_element_type=jnp.float32)
        for k in range(TILE // PAIR):
            piece = tile[:, k * PAIR : (k + 1) * PAIR].astype(jnp.bfloat16)
            keys[(TILE // PAIR) * i + k, 0:rows] = piece

    loads[5].wait()

    @pl.loop(0, qw // TILE)
    def _(i):
        at = pl.ds(pl.multiple_of(qw + i * TILE, TILE), TILE)
        tile = jnp.dot(modulated[...], wkv[:, at], preferred_element_type=jnp.float32)
        tile = tile.T.astype(jnp.bfloat16)
        for k in range(TILE // PAIR):
            values[(TILE // PAIR) * i + k, 0] = tile[k * PAIR : (k + 1) * PAIR]

    def attend(g, slot, slots, first, final):
        scores = jnp.dot(
            keys[g, pl.ds(slot * rows, slots * rows)], queries[g],
            preferred_element_type=jnp.float32,
        )
        top = jnp.max(scores, axis=0, keepdims=True)
        if not first:
            top = jnp.maximum(maxima[g], top)
        probs = jnp.exp(scores - top)
        total = jnp.sum(probs, axis=0, keepdims=True)
        if not first:
            kept = jnp.exp(maxima[g] - top)
            total = totals[g] * kept + total
        weights = probs.astype(jnp.bfloat16)
        heads = []
        for head in range(2):
            lanes = slice(head * rows, (head + 1) * rows)
            span = slice(head * HEAD_DIM, (head + 1) * HEAD_DIM)
            summed = running[g, span] * kept[:, lanes] if not first else None
            for k in range(slots):
                share = jnp.dot(
                    values[g, slot + k, span], weights[k * rows : (k + 1) * rows, lanes],
                    preferred_element_type=jnp.float32,
                )
                summed = share if summed is None else summed + share
            heads.append(summed / total[:, lanes] if final else summed)
        both = jnp.concatenate(heads, axis=0)
        if final:
            attention[:, columns(g)] = both.T.astype(jnp.bfloat16)
        else:
            maxima[g], totals[g], running[g] = top, total, both

    def attend_local(start, stop):
        @pl.loop(start, stop)
        def _(g):
            for part in range(2):
                to_sibling(g, part).wait_recv()
            attend(g, 0, 2, True, chips == 1)

    def attend_remote(g, together):
        for j in range(1, chips):
            if not together:
                attend(g, 2 * j, 1, False, False)
            for part in range(2):
                forward(j, g, part).wait_recv()
            if together:
                attend(g, 2 * j, 2, False, j == chips - 1)
            else:
                attend(g, 2 * j + 1, 1, False, j == chips - 1)

    advance(0)
    attend_local(0, pairs // 2)
    advance(1)
    attend_local(pairs // 2, pairs)
    advance(2)
    last = TILE // PAIR
    early = qw - TILE

    @pl.loop(0, 3)
    def _(g):
        attend_remote(g, True)

    @pl.loop(3, pairs - last)
    def _(g):
        advance(g)
        attend_remote(g, False)

    for load in loads[6:]:
        load.wait()
    wf_rows[...] = flip(wf[...])

    @pl.loop(0, width // TILE)
    def _(i):
        at = pl.ds(pl.multiple_of(i * TILE, TILE), TILE)
        tile = jnp.dot(
            attention[:, pl.ds(0, early)], wo[pl.ds(0, early), at],
            preferred_element_type=jnp.float32,
        )
        combined[:, at] = hidden[:, at].astype(jnp.float32) + gate[:, at] * tile

    @pl.loop(pairs - last, pairs)
    def _(g):
        advance(g)
        attend_remote(g, False)

    for i in range(width // TILE):
        at = pl.ds(i * TILE, TILE)
        tile = jnp.dot(
            attention[:, pl.ds(early, TILE)], wo[pl.ds(early, TILE), at],
            preferred_element_type=jnp.float32,
        )
        combined[:, at] += gate[:, at] * tile

    def seam(half):
        at = pl.ds(half * (rows // 2), rows // 2)
        return pltpu.make_async_remote_copy(
            src_ref=sent.at[:, at],
            dst_ref=other_hbm.at[:, at],
            send_sem=seam_send.at[half],
            recv_sem=seam_recv.at[half],
            device_id=partner,
            device_id_type=MESH,
        )

    for half in range(2):
        first = half * (rows // 2)
        for start in range(first, first + rows // 2, LN_ROWS):
            at = pl.ds(start, LN_ROWS)
            normed[at, :] = layer_norm(combined[at, :]).astype(jnp.bfloat16)
        at = pl.ds(first, rows // 2)
        velocity = jnp.dot(normed[at, :], wf_rows[...], preferred_element_type=jnp.float32)
        moved = latent[:, at] + step[0] * velocity.T
        advanced[:, at] = moved
        sent[:, at] = moved.astype(jnp.bfloat16)

        @pl.when(has_partner)
        def _():
            seam(half).start()

    keep = pltpu.make_async_copy(advanced, advanced_hbm, load_sem.at[len(loads)])
    keep.start()

    @pl.loop(0, pairs)
    def _(g):
        for part in range(2):
            to_sibling(g, part).wait_send()
            for j in range(1, chips):
                forward(j, g, part).wait_send()

    keep.wait()

    @pl.when(has_partner)
    def _():
        for half in range(2):
            seam(half).wait()


def on_device(
    windows,
    frame_devs,
    hidden_state,
    latent,
    stale_kv,
    mod_shift,
    mod_scale,
    mod_gate,
    w_query,
    w_keyval,
    w_out,
    w_final,
    step_size,
):
    rows, width = hidden_state.shape
    channels = latent.shape[1]
    qw = w_query.shape[1]
    pairs = qw // PAIR
    bf16, f32 = jnp.bfloat16, jnp.float32
    anywhere = pl.BlockSpec(memory_space=pl.ANY)
    advanced, other = pl.pallas_call(
        functools.partial(kernel, windows, frame_devs),
        out_shape=[jax.ShapeDtypeStruct((channels, rows), dtype) for dtype in (f32, bf16)],
        in_specs=[anywhere] + [pl.BlockSpec(memory_space=pltpu.HBM)] * 10,
        out_specs=[anywhere] * 2,
        scratch_shapes=[
            pltpu.SMEM((1,), f32),
            pltpu.VMEM((rows, width), bf16),
            pltpu.VMEM((channels, rows), f32),
            pltpu.VMEM((1, width), f32),
            pltpu.VMEM((1, width), f32),
            pltpu.VMEM((1, width), f32),
            pltpu.VMEM(w_query.shape, bf16),
            pltpu.VMEM(w_keyval.shape, bf16),
            pltpu.VMEM(w_out.shape, bf16),
            pltpu.VMEM((channels, width), bf16),
            pltpu.VMEM((width, channels), bf16),
            pltpu.VMEM((rows, width), bf16),
            pltpu.VMEM((pairs, PAIR, 2 * rows), bf16),
            pltpu.VMEM((2 * pairs, rows, PAIR), bf16),
            pltpu.VMEM((pairs, PAIR, rows), bf16),
            pltpu.VMEM((pairs, frame_devs * rows, PAIR), bf16),
            pltpu.VMEM((pairs, frame_devs, PAIR, rows), bf16),
            pltpu.VMEM((rows, qw), bf16),
            pltpu.VMEM((pairs, 1, 2 * rows), f32),
            pltpu.VMEM((pairs, 1, 2 * rows), f32),
            pltpu.VMEM((pairs, PAIR, rows), f32),
            pltpu.VMEM((rows, width), f32),
            pltpu.VMEM((rows, width), bf16),
            pltpu.VMEM((channels, rows), f32),
            pltpu.VMEM((channels, rows), bf16),
            pltpu.SemaphoreType.DMA((12,)),
            pltpu.SemaphoreType.DMA((pairs, 2)),
            pltpu.SemaphoreType.DMA((frame_devs, pairs, 2)),
            pltpu.SemaphoreType.DMA((frame_devs, pairs, 2)),
            pltpu.SemaphoreType.DMA((2,)),
            pltpu.SemaphoreType.DMA((2,)),
        ],
        compiler_params=pltpu.CompilerParams(
            collective_id=0, has_side_effects=True, vmem_limit_bytes=44 * 1024 * 1024
        ),
        name="dit_window_step",
    )(
        step_size,
        *(
            pltpu.with_memory_space_constraint(operand, pltpu.HBM)
            for operand in (
                hidden_state,
                latent.T,
                stale_kv,
                mod_shift,
                mod_scale,
                mod_gate,
                w_query,
                w_keyval,
                w_out,
                w_final.T,
            )
        )
    )
    w, f = lax.axis_index("win"), lax.axis_index("frm")
    half_devs = frame_devs // 2
    in_tail = f >= half_devs
    has_partner = jnp.where(in_tail, w < windows - 1, w > 0)
    first = jnp.where(in_tail, f - half_devs, f) * rows
    place = first + lax.broadcasted_iota(jnp.int32, (channels, rows), 1)
    ramp = (place.astype(f32) + 0.5) / (half_devs * rows)
    own = jnp.where(in_tail, 1.0 - ramp, ramp)
    blended = jnp.where(has_partner, own * advanced + (1.0 - own) * other, advanced)
    return blended.T


def solution(mesh):
    placed = (
        P(("win", "frm"), None),
        P(("win", "frm"), None),
        P(("win", "frm"), None),
        P("win", None),
        P("win", None),
        P("win", None),
        P(),
        P(),
        P(),
        P(),
        P("win"),
    )
    return jax.shard_map(
        functools.partial(on_device, mesh.shape["win"], mesh.shape["frm"]),
        mesh=mesh,
        in_specs=placed,
        out_specs=P(("win", "frm"), None),
        check_vma=False,
    )
```

```python
import functools

import jax
import jax.numpy as jnp
from jax import lax
from jax.experimental import pallas as pl
from jax.experimental.pallas import tpu as pltpu
from jax.sharding import PartitionSpec as P

HEAD_DIM = 64
AHEAD = 4
PAIR = 2 * HEAD_DIM
TILE = 256
LN_ROWS = 64
MESH = pl.DeviceIdType.MESH


def layer_norm(values):
    average = jnp.mean(values, axis=-1, keepdims=True)
    centred = values - average
    variance = jnp.mean(centred * centred, axis=-1, keepdims=True)
    return centred * lax.rsqrt(variance + 1e-06)


def flip(block):
    return block.astype(jnp.float32).T.astype(block.dtype)


def kernel(
    windows,
    frame_devs,
    step_hbm,
    hidden_hbm,
    latent_hbm,
    stale_hbm,
    shift_hbm,
    scale_hbm,
    gate_hbm,
    wq_hbm,
    wkv_hbm,
    wo_hbm,
    wf_hbm,
    advanced_hbm,
    other_hbm,
    step,
    hidden,
    latent,
    shift,
    scale,
    gate,
    wq,
    wkv,
    wo,
    wf,
    wf_rows,
    modulated,
    queries,
    staged,
    own,
    keys,
    values,
    attention,
    maxima,
    totals,
    running,
    combined,
    normed,
    advanced,
    sent,
    load_sem,
    stage_sem,
    send_sem,
    recv_sem,
    seam_send,
    seam_recv,
):
    rows, width = hidden.shape
    qw = wq.shape[1]
    pairs = qw // PAIR
    chips = frame_devs // 2
    half_devs = frame_devs // 2
    w = lax.axis_index("win")
    f = lax.axis_index("frm")
    chip, core = f // 2, f % 2
    sibling = (w, chip * 2 + (1 - core))
    peers = [(w, ((chip + j) % chips) * 2 + core) for j in range(1, chips)]
    in_tail = f >= half_devs
    has_partner = jnp.where(in_tail, w < windows - 1, w > 0)
    partner = (
        jnp.where(in_tail, w + 1, w - 1),
        jnp.where(in_tail, f - half_devs, f + half_devs),
    )

    loads = [
        pltpu.make_async_copy(src, dst, load_sem.at[i])
        for i, (src, dst) in enumerate(
            [
                (hidden_hbm, hidden),
                (scale_hbm, scale),
                (shift_hbm, shift),
                (wq_hbm, wq),
                (wkv_hbm.at[:, pl.ds(0, qw)], wkv.at[:, pl.ds(0, qw)]),
                (wkv_hbm.at[:, pl.ds(qw, qw)], wkv.at[:, pl.ds(qw, qw)]),
                (gate_hbm, gate),
                (wo_hbm, wo),
                (wf_hbm, wf),
                (latent_hbm, latent),
                (step_hbm, step),
            ]
        )
    ]
    def stage(g, part):
        at = pl.ds(pl.multiple_of(part * qw + g * PAIR, PAIR), PAIR)
        return pltpu.make_async_copy(
            stale_hbm.at[:, at], staged.at[part * pairs + g], stage_sem.at[g, part]
        )

    @pl.loop(0, pairs)
    def _(g):
        for part in range(2):
            stage(g, part).start()

    for load in loads:
        load.start()

    barrier = pltpu.get_barrier_semaphore()
    for device in [sibling] + peers:
        pl.semaphore_signal(barrier, inc=1, device_id=device, device_id_type=MESH)

    @pl.when(has_partner)
    def _():
        pl.semaphore_signal(barrier, inc=1, device_id=partner, device_id_type=MESH)

    pl.semaphore_wait(barrier, jnp.where(has_partner, chips + 1, chips))

    def columns(g):
        return pl.ds(g * PAIR, PAIR)

    def place(slot, g, part):
        return values.at[g, slot] if part else keys.at[g, pl.ds(slot * rows, rows)]

    def source(g, part):
        return own.at[g] if part else staged.at[g]

    def send(ref, slot, device, g, part):
        return pltpu.make_async_remote_copy(
            src_ref=ref,
            dst_ref=place(slot, g, part),
            send_sem=send_sem.at[slot, g, part],
            recv_sem=recv_sem.at[slot, g, part],
            device_id=device,
            device_id_type=MESH,
        )

    def to_sibling(g, part):
        return send(source(g, part), 1, sibling, g, part)

    def to_peer(j, g, part):
        return send(source(g, part), 2 * j, peers[j - 1], g, part)

    def forward(j, g, part):
        return send(place(2 * j, g, part), 2 * j + 1, sibling, g, part)

    def launch(g, part):
        for j in range(1, chips):
            to_peer(j, g, part).start()

    def arrive(g):
        for j in range(1, chips):
            for part in range(2):
                to_peer(j, g, part).wait_recv()
                forward(j, g, part).start()

    @pl.loop(0, pairs)
    def _(g):
        for part in range(2):
            stage(g, part).wait()
            if part:
                own[g] = flip(staged[pairs + g])

            @pl.when(g < AHEAD)
            def _():
                launch(g, part)

            to_sibling(g, part).start()

    def advance(g):
        arrive(g)
        if g + AHEAD < pairs:
            for part in range(2):
                launch(g + AHEAD, part)

    for load in loads[:3]:
        load.wait()

    for start in range(0, rows, LN_ROWS):
        at = pl.ds(start, LN_ROWS)
        line = layer_norm(hidden[at, :].astype(jnp.float32))
        modulated[at, :] = (line * (1.0 + scale[...]) + shift[...]).astype(jnp.bfloat16)

    loads[3].wait()
    blank = jnp.zeros((HEAD_DIM, rows), jnp.bfloat16)

    for i in range(qw // TILE):
        at = pl.ds(i * TILE, TILE)
        tile = jnp.dot(modulated[...], wq[:, at], preferred_element_type=jnp.float32)
        tile = (tile * HEAD_DIM ** (-0.5)).T.astype(jnp.bfloat16)
        for k in range(TILE // PAIR):
            g = (TILE // PAIR) * i + k
            first, second = k * PAIR, k * PAIR + HEAD_DIM
            queries[g, 0:HEAD_DIM, 0:rows] = tile[first:second]
            queries[g, HEAD_DIM:PAIR, 0:rows] = blank
            queries[g, 0:HEAD_DIM, rows : 2 * rows] = blank
            queries[g, HEAD_DIM:PAIR, rows : 2 * rows] = tile[second : second + HEAD_DIM]

    loads[4].wait()

    for i in range(qw // TILE):
        at = pl.ds(i * TILE, TILE)
        tile = jnp.dot(modulated[...], wkv[:, at], preferred_element_type=jnp.float32)
        for k in range(TILE // PAIR):
            piece = tile[:, k * PAIR : (k + 1) * PAIR].astype(jnp.bfloat16)
            keys[(TILE // PAIR) * i + k, 0:rows] = piece

    loads[5].wait()

    for i in range(qw // TILE):
        at = pl.ds(qw + i * TILE, TILE)
        tile = jnp.dot(modulated[...], wkv[:, at], preferred_element_type=jnp.float32)
        tile = tile.T.astype(jnp.bfloat16)
        for k in range(TILE // PAIR):
            values[(TILE // PAIR) * i + k, 0] = tile[k * PAIR : (k + 1) * PAIR]

    def attend(g, slot, slots, first, final):
        scores = jnp.dot(
            keys[g, pl.ds(slot * rows, slots * rows)], queries[g],
            preferred_element_type=jnp.float32,
        )
        top = jnp.max(scores, axis=0, keepdims=True)
        if not first:
            top = jnp.maximum(maxima[g], top)
        probs = jnp.exp(scores - top)
        total = jnp.sum(probs, axis=0, keepdims=True)
        if not first:
            kept = jnp.exp(maxima[g] - top)
            total = totals[g] * kept + total
        weights = probs.astype(jnp.bfloat16)
        heads = []
        for head in range(2):
            lanes = slice(head * rows, (head + 1) * rows)
            span = slice(head * HEAD_DIM, (head + 1) * HEAD_DIM)
            summed = running[g, span] * kept[:, lanes] if not first else None
            for k in range(slots):
                share = jnp.dot(
                    values[g, slot + k, span], weights[k * rows : (k + 1) * rows, lanes],
                    preferred_element_type=jnp.float32,
                )
                summed = share if summed is None else summed + share
            heads.append(summed / total[:, lanes] if final else summed)
        both = jnp.concatenate(heads, axis=0)
        if final:
            attention[:, columns(g)] = both.T.astype(jnp.bfloat16)
        else:
            maxima[g], totals[g], running[g] = top, total, both

    def attend_local(span):
        for g in span:
            for part in range(2):
                to_sibling(g, part).wait_recv()
        for g in span:
            attend(g, 0, 2, True, chips == 1)

    def attend_remote(span, together):
        for j in range(1, chips):
            final = j == chips - 1
            if not together:
                for g in span:
                    attend(g, 2 * j, 1, False, False)
            for g in span:
                for part in range(2):
                    forward(j, g, part).wait_recv()
            for g in span:
                if together:
                    attend(g, 2 * j, 2, False, final)
                else:
                    attend(g, 2 * j + 1, 1, False, final)

    last = TILE // PAIR
    early = qw - TILE
    half = pairs // 2
    advance(0)
    attend_local(range(half))
    advance(1)
    attend_local(range(half, pairs))
    advance(2)
    attend_remote(range(half), True)
    for g in range(half, pairs - last):
        advance(g)
        attend_remote([g], False)

    for load in loads[6:]:
        load.wait()
    wf_rows[...] = flip(wf[...])

    for i in range(width // TILE):
        at = pl.ds(i * TILE, TILE)
        tile = jnp.dot(
            attention[:, pl.ds(0, early)], wo[pl.ds(0, early), at],
            preferred_element_type=jnp.float32,
        )
        combined[:, at] = hidden[:, at].astype(jnp.float32) + gate[:, at] * tile

    for g in range(pairs - last, pairs):
        advance(g)
        attend_remote([g], False)

    for i in range(width // TILE):
        at = pl.ds(i * TILE, TILE)
        tile = jnp.dot(
            attention[:, pl.ds(early, TILE)], wo[pl.ds(early, TILE), at],
            preferred_element_type=jnp.float32,
        )
        combined[:, at] += gate[:, at] * tile

    def seam(half):
        at = pl.ds(half * (rows // 2), rows // 2)
        return pltpu.make_async_remote_copy(
            src_ref=sent.at[:, at],
            dst_ref=other_hbm.at[:, at],
            send_sem=seam_send.at[half],
            recv_sem=seam_recv.at[half],
            device_id=partner,
            device_id_type=MESH,
        )

    for half in range(2):
        first = half * (rows // 2)
        for start in range(first, first + rows // 2, LN_ROWS):
            at = pl.ds(start, LN_ROWS)
            normed[at, :] = layer_norm(combined[at, :]).astype(jnp.bfloat16)
        at = pl.ds(first, rows // 2)
        velocity = jnp.dot(normed[at, :], wf_rows[...], preferred_element_type=jnp.float32)
        moved = latent[:, at] + step[0] * velocity.T
        advanced[:, at] = moved
        sent[:, at] = moved.astype(jnp.bfloat16)

        @pl.when(has_partner)
        def _():
            seam(half).start()

    keep = pltpu.make_async_copy(advanced, advanced_hbm, load_sem.at[len(loads)])
    keep.start()

    @pl.loop(0, pairs)
    def _(g):
        for part in range(2):
            to_sibling(g, part).wait_send()
            for j in range(1, chips):
                to_peer(j, g, part).wait_send()
                forward(j, g, part).wait_send()

    keep.wait()

    @pl.when(has_partner)
    def _():
        for half in range(2):
            seam(half).wait()


def on_device(
    windows,
    frame_devs,
    hidden_state,
    latent,
    stale_kv,
    mod_shift,
    mod_scale,
    mod_gate,
    w_query,
    w_keyval,
    w_out,
    w_final,
    step_size,
):
    rows, width = hidden_state.shape
    channels = latent.shape[1]
    qw = w_query.shape[1]
    pairs = qw // PAIR
    bf16, f32 = jnp.bfloat16, jnp.float32
    anywhere = pl.BlockSpec(memory_space=pl.ANY)
    advanced, other = pl.pallas_call(
        functools.partial(kernel, windows, frame_devs),
        out_shape=[jax.ShapeDtypeStruct((channels, rows), dtype) for dtype in (f32, bf16)],
        in_specs=[anywhere] + [pl.BlockSpec(memory_space=pltpu.HBM)] * 10,
        out_specs=[anywhere] * 2,
        scratch_shapes=[
            pltpu.SMEM((1,), f32),
            pltpu.VMEM((rows, width), bf16),
            pltpu.VMEM((channels, rows), f32),
            pltpu.VMEM((1, width), f32),
            pltpu.VMEM((1, width), f32),
            pltpu.VMEM((1, width), f32),
            pltpu.VMEM(w_query.shape, bf16),
            pltpu.VMEM(w_keyval.shape, bf16),
            pltpu.VMEM(w_out.shape, bf16),
            pltpu.VMEM((channels, width), bf16),
            pltpu.VMEM((width, channels), bf16),
            pltpu.VMEM((rows, width), bf16),
            pltpu.VMEM((pairs, PAIR, 2 * rows), bf16),
            pltpu.VMEM((2 * pairs, rows, PAIR), bf16),
            pltpu.VMEM((pairs, PAIR, rows), bf16),
            pltpu.VMEM((pairs, frame_devs * rows, PAIR), bf16),
            pltpu.VMEM((pairs, frame_devs, PAIR, rows), bf16),
            pltpu.VMEM((rows, qw), bf16),
            pltpu.VMEM((pairs, 1, 2 * rows), f32),
            pltpu.VMEM((pairs, 1, 2 * rows), f32),
            pltpu.VMEM((pairs, PAIR, rows), f32),
            pltpu.VMEM((rows, width), f32),
            pltpu.VMEM((rows, width), bf16),
            pltpu.VMEM((channels, rows), f32),
            pltpu.VMEM((channels, rows), bf16),
            pltpu.SemaphoreType.DMA((12,)),
            pltpu.SemaphoreType.DMA((pairs, 2)),
            pltpu.SemaphoreType.DMA((frame_devs, pairs, 2)),
            pltpu.SemaphoreType.DMA((frame_devs, pairs, 2)),
            pltpu.SemaphoreType.DMA((2,)),
            pltpu.SemaphoreType.DMA((2,)),
        ],
        compiler_params=pltpu.CompilerParams(
            collective_id=0, has_side_effects=True, vmem_limit_bytes=44 * 1024 * 1024
        ),
        name="dit_window_step",
    )(
        step_size,
        *(
            pltpu.with_memory_space_constraint(operand, pltpu.HBM)
            for operand in (
                hidden_state,
                latent.T,
                stale_kv,
                mod_shift,
                mod_scale,
                mod_gate,
                w_query,
                w_keyval,
                w_out,
                w_final.T,
            )
        )
    )
    w, f = lax.axis_index("win"), lax.axis_index("frm")
    half_devs = frame_devs // 2
    in_tail = f >= half_devs
    has_partner = jnp.where(in_tail, w < windows - 1, w > 0)
    first = jnp.where(in_tail, f - half_devs, f) * rows
    place = first + lax.broadcasted_iota(jnp.int32, (channels, rows), 1)
    ramp = (place.astype(f32) + 0.5) / (half_devs * rows)
    own = jnp.where(in_tail, 1.0 - ramp, ramp)
    blended = jnp.where(has_partner, own * advanced + (1.0 - own) * other, advanced)
    return blended.T


def solution(mesh):
    placed = (
        P(("win", "frm"), None),
        P(("win", "frm"), None),
        P(("win", "frm"), None),
        P("win", None),
        P("win", None),
        P("win", None),
        P(),
        P(),
        P(),
        P(),
        P("win"),
    )
    return jax.shard_map(
        functools.partial(on_device, mesh.shape["win"], mesh.shape["frm"]),
        mesh=mesh,
        in_specs=placed,
        out_specs=P(("win", "frm"), None),
        check_vma=False,
    )
```

```python
import functools

import jax
import jax.numpy as jnp
from jax import lax
from jax.experimental import pallas as pl
from jax.experimental.pallas import tpu as pltpu
from jax.sharding import PartitionSpec as P

HEAD_DIM = 64
AHEAD = 6
PAIR = 2 * HEAD_DIM
TILE = 256
LN_ROWS = 64
MESH = pl.DeviceIdType.MESH


def layer_norm(values):
    average = jnp.mean(values, axis=-1, keepdims=True)
    centred = values - average
    variance = jnp.mean(centred * centred, axis=-1, keepdims=True)
    return centred * lax.rsqrt(variance + 1e-06)


def flip(block):
    return block.astype(jnp.float32).T.astype(block.dtype)


def kernel(
    windows,
    frame_devs,
    step_hbm,
    hidden_hbm,
    latent_hbm,
    stale_hbm,
    shift_hbm,
    scale_hbm,
    gate_hbm,
    wq_hbm,
    wkv_hbm,
    wo_hbm,
    wf_hbm,
    advanced_hbm,
    other_hbm,
    step,
    hidden,
    latent,
    shift,
    scale,
    gate,
    wq,
    wkv,
    wo,
    wf,
    wf_rows,
    modulated,
    queries,
    staged,
    own,
    keys,
    values,
    attention,
    maxima,
    totals,
    running,
    combined,
    normed,
    advanced,
    sent,
    load_sem,
    stage_sem,
    send_sem,
    recv_sem,
    seam_send,
    seam_recv,
):
    rows, width = hidden.shape
    qw = wq.shape[1]
    pairs = qw // PAIR
    chips = frame_devs // 2
    half_devs = frame_devs // 2
    w = lax.axis_index("win")
    f = lax.axis_index("frm")
    chip, core = f // 2, f % 2
    sibling = (w, chip * 2 + (1 - core))
    peers = [(w, ((chip + j) % chips) * 2 + core) for j in range(1, chips)]
    in_tail = f >= half_devs
    has_partner = jnp.where(in_tail, w < windows - 1, w > 0)
    partner = (
        jnp.where(in_tail, w + 1, w - 1),
        jnp.where(in_tail, f - half_devs, f + half_devs),
    )

    loads = [
        pltpu.make_async_copy(src, dst, load_sem.at[i])
        for i, (src, dst) in enumerate(
            [
                (hidden_hbm, hidden),
                (scale_hbm, scale),
                (shift_hbm, shift),
                (wq_hbm, wq),
                (wkv_hbm.at[:, pl.ds(0, qw)], wkv.at[:, pl.ds(0, qw)]),
                (wkv_hbm.at[:, pl.ds(qw, qw)], wkv.at[:, pl.ds(qw, qw)]),
                (gate_hbm, gate),
                (wo_hbm, wo),
                (wf_hbm, wf),
                (latent_hbm, latent),
                (step_hbm, step),
            ]
        )
    ]
    def stage(g, part):
        at = pl.ds(pl.multiple_of(part * qw + g * PAIR, PAIR), PAIR)
        return pltpu.make_async_copy(
            stale_hbm.at[:, at], staged.at[part * pairs + g], stage_sem.at[g, part]
        )

    @pl.loop(0, pairs)
    def _(g):
        for part in range(2):
            stage(g, part).start()

    for load in loads:
        load.start()

    barrier = pltpu.get_barrier_semaphore()
    for device in [sibling] + peers:
        pl.semaphore_signal(barrier, inc=1, device_id=device, device_id_type=MESH)

    @pl.when(has_partner)
    def _():
        pl.semaphore_signal(barrier, inc=1, device_id=partner, device_id_type=MESH)

    pl.semaphore_wait(barrier, jnp.where(has_partner, chips + 1, chips))

    def columns(g):
        return pl.ds(g * PAIR, PAIR)

    def place(slot, g, part):
        return values.at[g, slot] if part else keys.at[g, pl.ds(slot * rows, rows)]

    def source(g, part):
        return own.at[g] if part else staged.at[g]

    def send(ref, slot, device, g, part):
        return pltpu.make_async_remote_copy(
            src_ref=ref,
            dst_ref=place(slot, g, part),
            send_sem=send_sem.at[slot, g, part],
            recv_sem=recv_sem.at[slot, g, part],
            device_id=device,
            device_id_type=MESH,
        )

    def to_sibling(g, part):
        return send(source(g, part), 1, sibling, g, part)

    def to_peer(j, g, part):
        return send(source(g, part), 2 * j, peers[j - 1], g, part)

    def forward(j, g, part):
        return send(place(2 * j, g, part), 2 * j + 1, sibling, g, part)

    def launch(g, part):
        for j in range(1, chips):
            to_peer(j, g, part).start()

    def arrive(g):
        for j in range(1, chips):
            for part in range(2):
                to_peer(j, g, part).wait_recv()
                forward(j, g, part).start()

    @pl.loop(0, pairs)
    def _(g):
        for part in range(2):
            stage(g, part).wait()
            if part:
                own[g] = flip(staged[pairs + g])

            @pl.when(g < AHEAD)
            def _():
                launch(g, part)

            to_sibling(g, part).start()

    def advance(g):
        arrive(g)
        if g + AHEAD < pairs:
            for part in range(2):
                launch(g + AHEAD, part)

    for load in loads[:3]:
        load.wait()

    for start in range(0, rows, LN_ROWS):
        at = pl.ds(start, LN_ROWS)
        line = layer_norm(hidden[at, :].astype(jnp.float32))
        modulated[at, :] = (line * (1.0 + scale[...]) + shift[...]).astype(jnp.bfloat16)

    loads[3].wait()
    blank = jnp.zeros((HEAD_DIM, rows), jnp.bfloat16)

    for i in range(qw // TILE):
        at = pl.ds(i * TILE, TILE)
        tile = jnp.dot(modulated[...], wq[:, at], preferred_element_type=jnp.float32)
        tile = (tile * HEAD_DIM ** (-0.5)).T.astype(jnp.bfloat16)
        for k in range(TILE // PAIR):
            g = (TILE // PAIR) * i + k
            first, second = k * PAIR, k * PAIR + HEAD_DIM
            queries[g, 0:HEAD_DIM, 0:rows] = tile[first:second]
            queries[g, HEAD_DIM:PAIR, 0:rows] = blank
            queries[g, 0:HEAD_DIM, rows : 2 * rows] = blank
            queries[g, HEAD_DIM:PAIR, rows : 2 * rows] = tile[second : second + HEAD_DIM]

    loads[4].wait()

    for i in range(qw // TILE):
        at = pl.ds(i * TILE, TILE)
        tile = jnp.dot(modulated[...], wkv[:, at], preferred_element_type=jnp.float32)
        for k in range(TILE // PAIR):
            piece = tile[:, k * PAIR : (k + 1) * PAIR].astype(jnp.bfloat16)
            keys[(TILE // PAIR) * i + k, 0:rows] = piece

    loads[5].wait()

    for i in range(qw // TILE):
        at = pl.ds(qw + i * TILE, TILE)
        tile = jnp.dot(modulated[...], wkv[:, at], preferred_element_type=jnp.float32)
        tile = tile.T.astype(jnp.bfloat16)
        for k in range(TILE // PAIR):
            values[(TILE // PAIR) * i + k, 0] = tile[k * PAIR : (k + 1) * PAIR]

    def attend(g, slot, slots, first, final):
        scores = jnp.dot(
            keys[g, pl.ds(slot * rows, slots * rows)], queries[g],
            preferred_element_type=jnp.float32,
        )
        top = jnp.max(scores, axis=0, keepdims=True)
        if not first:
            top = jnp.maximum(maxima[g], top)
        probs = jnp.exp(scores - top)
        total = jnp.sum(probs, axis=0, keepdims=True)
        if not first:
            kept = jnp.exp(maxima[g] - top)
            total = totals[g] * kept + total
        weights = probs.astype(jnp.bfloat16)
        heads = []
        for head in range(2):
            lanes = slice(head * rows, (head + 1) * rows)
            span = slice(head * HEAD_DIM, (head + 1) * HEAD_DIM)
            summed = running[g, span] * kept[:, lanes] if not first else None
            for k in range(slots):
                share = jnp.dot(
                    values[g, slot + k, span], weights[k * rows : (k + 1) * rows, lanes],
                    preferred_element_type=jnp.float32,
                )
                summed = share if summed is None else summed + share
            heads.append(summed / total[:, lanes] if final else summed)
        both = jnp.concatenate(heads, axis=0)
        if final:
            attention[:, columns(g)] = both.T.astype(jnp.bfloat16)
        else:
            maxima[g], totals[g], running[g] = top, total, both

    def attend_local(span):
        for g in span:
            for part in range(2):
                to_sibling(g, part).wait_recv()
        for g in span:
            attend(g, 0, 2, True, chips == 1)

    def attend_remote(span, together):
        for j in range(1, chips):
            final = j == chips - 1
            if not together:
                for g in span:
                    attend(g, 2 * j, 1, False, False)
            for g in span:
                for part in range(2):
                    forward(j, g, part).wait_recv()
            for g in span:
                if together:
                    attend(g, 2 * j, 2, False, final)
                else:
                    attend(g, 2 * j + 1, 1, False, final)

    last = TILE // PAIR
    early = qw - TILE
    half = pairs // 2
    advance(0)
    attend_local(range(half))
    advance(1)
    attend_local(range(half, pairs))
    advance(2)
    attend_remote(range(half), True)
    for g in range(half, pairs - last):
        advance(g)
        attend_remote([g], False)

    for load in loads[6:]:
        load.wait()
    wf_rows[...] = flip(wf[...])

    for i in range(width // TILE):
        at = pl.ds(i * TILE, TILE)
        tile = jnp.dot(
            attention[:, pl.ds(0, early)], wo[pl.ds(0, early), at],
            preferred_element_type=jnp.float32,
        )
        combined[:, at] = hidden[:, at].astype(jnp.float32) + gate[:, at] * tile

    for g in range(pairs - last, pairs):
        advance(g)
        attend_remote([g], False)

    for i in range(width // TILE):
        at = pl.ds(i * TILE, TILE)
        tile = jnp.dot(
            attention[:, pl.ds(early, TILE)], wo[pl.ds(early, TILE), at],
            preferred_element_type=jnp.float32,
        )
        combined[:, at] += gate[:, at] * tile

    def seam(half):
        at = pl.ds(half * (rows // 2), rows // 2)
        return pltpu.make_async_remote_copy(
            src_ref=sent.at[:, at],
            dst_ref=other_hbm.at[:, at],
            send_sem=seam_send.at[half],
            recv_sem=seam_recv.at[half],
            device_id=partner,
            device_id_type=MESH,
        )

    for half in range(2):
        first = half * (rows // 2)
        for start in range(first, first + rows // 2, LN_ROWS):
            at = pl.ds(start, LN_ROWS)
            normed[at, :] = layer_norm(combined[at, :]).astype(jnp.bfloat16)
        at = pl.ds(first, rows // 2)
        velocity = jnp.dot(normed[at, :], wf_rows[...], preferred_element_type=jnp.float32)
        moved = latent[:, at] + step[0] * velocity.T
        advanced[:, at] = moved
        sent[:, at] = moved.astype(jnp.bfloat16)

        @pl.when(has_partner)
        def _():
            seam(half).start()

    keep = pltpu.make_async_copy(advanced, advanced_hbm, load_sem.at[len(loads)])
    keep.start()

    @pl.loop(0, pairs)
    def _(g):
        for part in range(2):
            to_sibling(g, part).wait_send()
            for j in range(1, chips):
                to_peer(j, g, part).wait_send()
                forward(j, g, part).wait_send()

    keep.wait()

    @pl.when(has_partner)
    def _():
        for half in range(2):
            seam(half).wait()


def on_device(
    windows,
    frame_devs,
    hidden_state,
    latent,
    stale_kv,
    mod_shift,
    mod_scale,
    mod_gate,
    w_query,
    w_keyval,
    w_out,
    w_final,
    step_size,
):
    rows, width = hidden_state.shape
    channels = latent.shape[1]
    qw = w_query.shape[1]
    pairs = qw // PAIR
    bf16, f32 = jnp.bfloat16, jnp.float32
    anywhere = pl.BlockSpec(memory_space=pl.ANY)
    advanced, other = pl.pallas_call(
        functools.partial(kernel, windows, frame_devs),
        out_shape=[jax.ShapeDtypeStruct((channels, rows), dtype) for dtype in (f32, bf16)],
        in_specs=[anywhere] + [pl.BlockSpec(memory_space=pltpu.HBM)] * 10,
        out_specs=[anywhere] * 2,
        scratch_shapes=[
            pltpu.SMEM((1,), f32),
            pltpu.VMEM((rows, width), bf16),
            pltpu.VMEM((channels, rows), f32),
            pltpu.VMEM((1, width), f32),
            pltpu.VMEM((1, width), f32),
            pltpu.VMEM((1, width), f32),
            pltpu.VMEM(w_query.shape, bf16),
            pltpu.VMEM(w_keyval.shape, bf16),
            pltpu.VMEM(w_out.shape, bf16),
            pltpu.VMEM((channels, width), bf16),
            pltpu.VMEM((width, channels), bf16),
            pltpu.VMEM((rows, width), bf16),
            pltpu.VMEM((pairs, PAIR, 2 * rows), bf16),
            pltpu.VMEM((2 * pairs, rows, PAIR), bf16),
            pltpu.VMEM((pairs, PAIR, rows), bf16),
            pltpu.VMEM((pairs, frame_devs * rows, PAIR), bf16),
            pltpu.VMEM((pairs, frame_devs, PAIR, rows), bf16),
            pltpu.VMEM((rows, qw), bf16),
            pltpu.VMEM((pairs, 1, 2 * rows), f32),
            pltpu.VMEM((pairs, 1, 2 * rows), f32),
            pltpu.VMEM((pairs, PAIR, rows), f32),
            pltpu.VMEM((rows, width), f32),
            pltpu.VMEM((rows, width), bf16),
            pltpu.VMEM((channels, rows), f32),
            pltpu.VMEM((channels, rows), bf16),
            pltpu.SemaphoreType.DMA((12,)),
            pltpu.SemaphoreType.DMA((pairs, 2)),
            pltpu.SemaphoreType.DMA((frame_devs, pairs, 2)),
            pltpu.SemaphoreType.DMA((frame_devs, pairs, 2)),
            pltpu.SemaphoreType.DMA((2,)),
            pltpu.SemaphoreType.DMA((2,)),
        ],
        compiler_params=pltpu.CompilerParams(
            collective_id=0, has_side_effects=True, vmem_limit_bytes=44 * 1024 * 1024
        ),
        name="dit_window_step",
    )(
        step_size,
        *(
            pltpu.with_memory_space_constraint(operand, pltpu.HBM)
            for operand in (
                hidden_state,
                latent.T,
                stale_kv,
                mod_shift,
                mod_scale,
                mod_gate,
                w_query,
                w_keyval,
                w_out,
                w_final.T,
            )
        )
    )
    w, f = lax.axis_index("win"), lax.axis_index("frm")
    half_devs = frame_devs // 2
    in_tail = f >= half_devs
    has_partner = jnp.where(in_tail, w < windows - 1, w > 0)
    first = jnp.where(in_tail, f - half_devs, f) * rows
    place = first + lax.broadcasted_iota(jnp.int32, (channels, rows), 1)
    ramp = (place.astype(f32) + 0.5) / (half_devs * rows)
    own = jnp.where(in_tail, 1.0 - ramp, ramp)
    blended = jnp.where(has_partner, own * advanced + (1.0 - own) * other, advanced)
    return blended.T


def solution(mesh):
    placed = (
        P(("win", "frm"), None),
        P(("win", "frm"), None),
        P(("win", "frm"), None),
        P("win", None),
        P("win", None),
        P("win", None),
        P(),
        P(),
        P(),
        P(),
        P("win"),
    )
    return jax.shard_map(
        functools.partial(on_device, mesh.shape["win"], mesh.shape["frm"]),
        mesh=mesh,
        in_specs=placed,
        out_specs=P(("win", "frm"), None),
        check_vma=False,
    )
```
